128 devices in a mesh: gx: 4 (over x), gy: 32 (over y, z, core).
Axes of the slice: x: 4, y: 4, z: 4, core: 2. Of those that a mesh axis runs over, the one named last changes fastest.
Arguments:
- linearized_heat_field: float32 [32, 256, 128], P('gx', 'gy'), may hold values from -6 to 6
- local_rock_factor: float32 [32, 256, 128], P('gx', 'gy'), may hold values from 0.5 to 2
- misfit_heat_derivative: float32 [32, 256, 128], P('gx', 'gy'), may hold values from -6 to 6
- patch_region_map: int32 [32, 256, 1], P('gx', 'gy'), may hold values from 0 to 65535
- region_logarithmic_thermal: float32 [65536], P('gy'), may hold values from -2.5 to 2.5
- region_tally_per_rank: int32 [32], replicated, may hold values from 1 to 4096, 65536 in all
- region_adjacency_table: int32 [65536, 6], P('gy'), may hold values from 0 to 65535
Outputs:
- zone_gradient: float32 [131072], P('gy')
The draws below stay inside these ranges and needn't reach their ends.
Inputs may be any that keep to these rules, and one draw needn't show every extreme that they name: `region_tally_per_rank`: the counts sum to 65536; some owner holds exactly 4096 zones.
All inputs are finite; a program needn't handle non-finite values.
Results may differ from the reference program's by a relative error of at most 0.00002.
Values sent between devices are 32-bit elements; how exact they have to be, the bound alone decides.
No kernel may reach another device: no remote copies, remote signals or barrier semaphores. Data moves between devices by JAX's collectives and lax.ppermute only.
A program may use at most 64 MiB of HBM per device.

```python
import math
import jax
import jax.numpy as jnp
import numpy as np

VERTICAL_UNITS = 128
ZONES = 65536
NBRS = 6
ITERS = 3
EASTWARD_UNITS = 32
NORTHWARD_UNITS = 256
NB = 1
ZCAP = 4096
N_GY = 32


def plant(result, key, low, largest):
    spot = [jax.random.randint(jax.random.fold_in(key, axis), (), 0, length) for axis, length in enumerate(result.shape)]
    widest = result.shape.index(max(result.shape))
    next_to = spot[:widest] + [(spot[widest] + 1) % result.shape[widest]] + spot[widest + 1:]
    return result.at[tuple(spot)].set(low).at[tuple(next_to)].set(largest)


def block_levels(rng, shape, pieces, low, high):
    gain, own = 1.0, jax.random.fold_in(rng, 6)
    for position, shards_of in pieces:
        draws = jnp.exp(jax.random.uniform(jax.random.fold_in(own, position), (shards_of,), jnp.float32, low / len(pieces), high / len(pieces)))
        gain = gain * jnp.repeat(draws, shape[position] // shards_of).reshape([-1 if axis == position else 1 for axis in range(len(shape))])
    return gain


def profile(count, total, reach, skew):
    loads = [(1 << 20) // math.isqrt(standing ** skew) + 1 for standing in range(2, count + 1)]
    rest, given = total - reach - (count - 1), [1] * (count - 1)
    while rest > 0:
        candidates = [i for i in range(count - 1) if given[i] < reach]
        whole, left = sum([loads[i] for i in candidates]), rest
        for i in candidates:
            extra = min(reach - given[i], max(1, left * loads[i] // whole), rest)
            given[i] = given[i] + extra
            rest = rest - extra
    return np.array([reach] + given)


def uneven(stream_key, count, total, reach, skew):
    if count == 2:
        one = jax.random.randint(stream_key, (), max(1, total - reach), min(reach, total - 1) + 1)
        return jnp.stack([one, total - one])
    sizes = jnp.asarray(profile(count, total, reach, skew), jnp.int32)
    pairs = (count - 1) // 2
    donor, taker = sizes[1:1 + 2 * pairs:2], sizes[2:2 + 2 * pairs:2]
    margin = jnp.minimum(donor - 1, reach - taker)
    passed = jax.random.randint(jax.random.fold_in(stream_key, 1), (pairs,), 0, 1 << 20) % (margin + 1)
    sizes = sizes.at[1:1 + 2 * pairs:2].set(donor - passed).at[2:2 + 2 * pairs:2].set(taker + passed)
    return sizes[jax.random.permutation(jax.random.fold_in(stream_key, 2), count)]


def normal_values(key, dims, width, most, cuts=(), kind=jnp.bfloat16):
    level = block_levels(key, dims, cuts, -0.22, 0.18) if cuts else 1.0
    result = jax.random.normal(key, dims, jnp.float32) * width * level
    return jnp.minimum(jnp.maximum(result, -most), most).astype(kind)


def setup_inputs(seed: int = 0) -> dict:
    streams_of = jax.random.split(jax.random.key(seed), 8)
    linearized_heat_field = normal_values(streams_of[0], (EASTWARD_UNITS, NORTHWARD_UNITS, VERTICAL_UNITS), 1.0, 6.0, ((0, 4), (1, 32)), jnp.float32)
    local_rock_factor = jnp.clip(jnp.exp(math.log(2.0) - 1.3862944 * jax.random.uniform(streams_of[1], (EASTWARD_UNITS, NORTHWARD_UNITS, VERTICAL_UNITS), jnp.float32) ** block_levels(streams_of[1], (EASTWARD_UNITS, NORTHWARD_UNITS, VERTICAL_UNITS), ((0, 4), (1, 32)), -0.2, 0.2)), 0.5, 2.0)
    misfit_heat_derivative = normal_values(streams_of[2], (EASTWARD_UNITS, NORTHWARD_UNITS, VERTICAL_UNITS), 1.0, 6.0, ((0, 4), (1, 32)), jnp.float32)
    patch_region_map = plant(jax.random.randint(streams_of[3], (EASTWARD_UNITS, NORTHWARD_UNITS, NB), 0, ZONES), jax.random.fold_in(streams_of[3], 1), 0, ZONES - 1).astype(jnp.int32)
    region_logarithmic_thermal = normal_values(streams_of[4], (ZONES,), 0.5, 2.5, ((0, 32),), jnp.float32)
    region_tally_per_rank = uneven(streams_of[5], N_GY, ZONES, ZCAP, 2).astype(jnp.int32)
    region_adjacency_table = plant(jax.random.randint(streams_of[6], (ZONES, NBRS), 0, ZONES), jax.random.fold_in(streams_of[6], 1), 0, ZONES - 1).astype(jnp.int32)
    return {"linearized_heat_field": linearized_heat_field, "local_rock_factor": local_rock_factor, "misfit_heat_derivative": misfit_heat_derivative, "patch_region_map": patch_region_map, "region_logarithmic_thermal": region_logarithmic_thermal, "region_tally_per_rank": region_tally_per_rank, "region_adjacency_table": region_adjacency_table}


relaxation = 0.8
smoothing = 0.5
sens_scale = 0.03125


def hexa_face_offsets(padded):
    return (padded[2:, 1:-1, 1:-1], padded[:-2, 1:-1, 1:-1], padded[1:-1, 2:, 1:-1],
            padded[1:-1, :-2, 1:-1], padded[1:-1, 1:-1, 2:], padded[1:-1, 1:-1, :-2])


def conduct_parts(local_thermal_factor, padded_conduct):
    faces = tuple((local_thermal_factor + side) * 0.5 for side in hexa_face_offsets(padded_conduct))
    diagonal = faces[0] + faces[1] + faces[2] + faces[3] + faces[4] + faces[5]
    return faces, diagonal


def jacobi_step(dual_solution, dual_padded_field, faces, diagonal, source):
    sides = hexa_face_offsets(dual_padded_field)
    coupled = faces[0] * sides[0]
    for number in range(1, 6):
        coupled = coupled + faces[number] * sides[number]
    applied = diagonal * dual_solution - coupled
    return dual_solution + relaxation * (source - applied) / diagonal


def local_misfit_derivative(linearized_heat_field, heat_padded_field, dual_solution, dual_padded_field, local_thermal_factor):
    full_objective_derivative = jnp.zeros_like(linearized_heat_field)
    for heat_adjacent_values, dual_adjacent_values in zip(hexa_face_offsets(heat_padded_field), hexa_face_offsets(dual_padded_field)):
        full_objective_derivative = full_objective_derivative + (linearized_heat_field - heat_adjacent_values) * (dual_solution - dual_adjacent_values)
    return -0.5 * full_objective_derivative * local_thermal_factor


def reference(linearized_heat_field, local_rock_factor, misfit_heat_derivative, patch_region_map, region_logarithmic_thermal, region_tally_per_rank, region_adjacency_table):
    eastward_span, northward_span, vertical_layer_number = linearized_heat_field.shape
    blocks = patch_region_map.shape[2]
    zone_log = region_logarithmic_thermal[patch_region_map]
    local_thermal_factor = (local_rock_factor.reshape(eastward_span, northward_span, blocks, vertical_layer_number // blocks) * jnp.exp(zone_log)[..., None]).reshape(eastward_span, northward_span, vertical_layer_number)
    faces, diagonal = conduct_parts(local_thermal_factor, jnp.pad(local_thermal_factor, 1))
    dual_solution = misfit_heat_derivative / diagonal
    for sweep in range(ITERS):
        dual_solution = jacobi_step(dual_solution, jnp.pad(dual_solution, 1), faces, diagonal, misfit_heat_derivative)
    scaled_contributions = local_misfit_derivative(linearized_heat_field, jnp.pad(linearized_heat_field, 1), dual_solution, jnp.pad(dual_solution, 1), local_thermal_factor)
    block_sums = scaled_contributions.reshape(eastward_span, northward_span, blocks, vertical_layer_number // blocks).sum(-1)
    zone_sums = jax.ops.segment_sum(block_sums.reshape(-1), patch_region_map.reshape(-1), num_segments=ZONES)
    neighbour_sum = jnp.sum(region_logarithmic_thermal[region_adjacency_table], axis=-1)
    gradient = sens_scale * zone_sums + smoothing * (NBRS * region_logarithmic_thermal - neighbour_sum)
    slots = jnp.arange(N_GY * ZCAP, dtype=jnp.int32)
    owner = slots // ZCAP
    within = slots % ZCAP
    ends = jnp.cumsum(region_tally_per_rank).astype(jnp.int32)
    starts = ends - region_tally_per_rank
    zone = starts[owner] + within
    valid = within < region_tally_per_rank[owner]
    picked = gradient[jnp.minimum(zone, ZONES - 1)]
    return jnp.where(valid, picked, jnp.float32(0.0))
```

```python
import jax
import jax.numpy as jnp
from jax import lax
from jax.experimental import pallas as pl
from jax.experimental.pallas import tpu as pltpu
from jax.sharding import PartitionSpec as P

NBRS = 6
ITERS = 3
RELAXATION = 0.8
SMOOTHING = 0.5
SENS_SCALE = 0.03125
LANES = 128
F32 = jnp.float32
BF16 = jnp.bfloat16
I32 = jnp.int32

VMEM = pl.BlockSpec(memory_space=pltpu.VMEM)
SMEM = pl.BlockSpec(memory_space=pltpu.SMEM)


def iota(shape, dim):
    return lax.broadcasted_iota(I32, shape, dim)


def call(kernel, outs, in_specs, scratch=(), cost=None):
    one = not isinstance(outs, (list, tuple))
    shapes = [outs] if one else list(outs)
    return pl.pallas_call(
        kernel,
        out_shape=shapes[0] if one else shapes,
        in_specs=in_specs,
        out_specs=VMEM if one else [VMEM] * len(shapes),
        scratch_shapes=list(scratch),
        cost_estimate=cost,
        compiler_params=pltpu.CompilerParams(vmem_limit_bytes=32 << 20),
    )


def thirds(table):
    first = table.astype(BF16)
    rest = table - first.astype(F32)
    second = rest.astype(BF16)
    third = (rest - second.astype(F32)).astype(BF16)
    return first, second, third


def pack_kernel(temp_ref, rock_ref, misfit_ref, map_ref, zone_ref, pack_ref, spread_ref):
    pack_ref[0] = rock_ref[...]
    pack_ref[1] = misfit_ref[...]
    pack_ref[2] = temp_ref[...]
    east, north = rock_ref.shape[0], rock_ref.shape[1]
    diagonal = iota((north, north), 0) == iota((north, north), 1)
    for x in range(east):
        row = jnp.broadcast_to(map_ref[x].astype(F32), (north, north))
        column = jnp.sum(jnp.where(diagonal, row, 0.0), axis=1, keepdims=True)
        pack_ref[3, x] = jnp.broadcast_to(column, (north, LANES))
    shard = zone_ref[...]
    for other in range(spread_ref.shape[0]):
        spread_ref[other] = shard


def extend_kernel(own_ref, south_ref, north_ref, table_ref, ext_ref, low_ref, high_ref):
    east = own_ref.shape[1]

    def window(field):
        return jnp.concatenate([south_ref[field], own_ref[field], north_ref[field]], axis=1)

    ids = window(3).reshape(east * 24, LANES).astype(I32)
    rows = ids >> 7
    lane = iota((east * 24, LANES), 1)
    hot = jnp.concatenate(
        [jnp.where(rows == lane + LANES * part, 1.0, 0.0).astype(BF16) for part in range(table_ref.shape[0] // LANES)],
        axis=1,
    )
    found = sum(jnp.dot(hot, piece, preferred_element_type=F32) for piece in thirds(table_ref[...]))
    log = jnp.sum(jnp.where(lane == (ids & 127), found, 0.0), axis=1, keepdims=True)
    conduct = window(0) * jnp.exp(jnp.broadcast_to(log, (east * 24, LANES))).reshape(east, 24, LANES)
    inner = conduct[:, 4:20]
    misfit, temp = window(1)[:, 4:20], window(2)[:, 4:20]
    ext_ref[0] = inner
    ext_ref[1] = conduct[:, 3:19] + conduct[:, 5:21]
    ext_ref[2] = misfit
    ext_ref[3] = temp
    low_ref[0:5] = inner[0:5]
    low_ref[5:9] = misfit[0:4]
    low_ref[9:10] = temp[0:1]
    high_ref[0:5] = inner[3:8]
    high_ref[5:9] = misfit[4:8]
    high_ref[9:10] = temp[7:8]


def smooth_kernel(gx_ref, adjacency_ref, zone_ref, table_ref, after_ref, out_ref):
    rows = out_ref.shape[0]
    count = rows * LANES
    high_size = table_ref.shape[0]
    pieces = jnp.concatenate(thirds(jnp.transpose(table_ref[...])), axis=0)
    offset = pl.multiple_of(gx_ref[0] * count, count)
    high_row = iota((high_size, count), 0)
    low_row = iota((LANES, count), 0)
    total = jnp.zeros((LANES, count), F32)
    for k in range(NBRS):
        ids = adjacency_ref[k : k + 1, pl.ds(offset, count)]
        hot = jnp.where(high_row == (ids >> 7), 1.0, 0.0).astype(BF16)
        found = jnp.dot(pieces, hot, preferred_element_type=F32)
        found = found[0:LANES] + found[LANES : 2 * LANES] + found[2 * LANES :]
        total = total + jnp.where(low_row == (ids & 127), found, 0.0)
    near = jnp.sum(total, axis=0, keepdims=True)
    own = zone_ref[pl.ds(gx_ref[0] * rows, rows), :]
    for row in range(rows):
        out_ref[row : row + 1] = SMOOTHING * (
            NBRS * own[row : row + 1] - near[:, row * LANES : (row + 1) * LANES]
        )


def sweep_kernel(ext_ref, west_ref, east_ref, ids_ref, smooth_ref, out_ref):
    shape = (16, LANES)
    lane = iota(shape, 1)
    first, last = lane == 0, lane == LANES - 1

    def depth_sides(v):
        up = jnp.where(first, 0.0, pltpu.roll(v, 1, 1))
        down = jnp.where(last, 0.0, pltpu.roll(v, LANES - 1, 1))
        return up, down

    def north_sides(v):
        return pltpu.roll(v, 1, 0), pltpu.roll(v, 15, 0)

    def around(rows, x):
        v = rows[x]
        up, down = depth_sides(v)
        south, north = north_sides(v)
        return ((rows[x - 1] + rows[x + 1]) + (south + north)) + (up + down)

    conduct = {x: ext_ref[0, x] for x in range(8)}
    source = {x: ext_ref[2, x] for x in range(8)}
    heat = {x: ext_ref[3, x] for x in range(8)}
    for step in range(5):
        conduct[step - 5] = west_ref[step]
        conduct[step + 8] = east_ref[step]
    for step in range(4):
        source[step - 4] = west_ref[5 + step]
        source[step + 8] = east_ref[5 + step]
    heat[-1] = west_ref[9]
    heat[8] = east_ref[9]

    inverse, dual, flux = {}, {}, {}
    for x in range(-4, 12):
        v = conduct[x]
        if 0 <= x < 8:
            across = ext_ref[1, x]
        else:
            south, north = north_sides(v)
            across = south + north
        up, down = depth_sides(v)
        twice = 6.0 * v + (((conduct[x - 1] + conduct[x + 1]) + across) + (up + down))
        inverse[x] = jnp.where(v > 0.0, 2.0 / twice, 0.0)
        dual[x] = source[x] * inverse[x]
    for sweep in range(ITERS):
        reach = 3 - sweep
        flux = {x: conduct[x] * dual[x] for x in dual}
        fresh = {}
        for x in range(-reach, 8 + reach):
            coupled = 0.5 * (conduct[x] * around(dual, x) + around(flux, x))
            fresh[x] = (1.0 - RELAXATION) * dual[x] + (RELAXATION * inverse[x]) * (source[x] + coupled)
        dual = fresh
    blocks = []
    for x in range(8):
        t, v = heat[x], dual[x]
        total = (t - heat[x + 1]) * (v - dual[x + 1]) + (t - heat[x - 1]) * (v - dual[x - 1])
        for near_t, near_v in zip(north_sides(t) + depth_sides(t), north_sides(v) + depth_sides(v)):
            total = total + (t - near_t) * (v - near_v)
        blocks.append(((-0.5 * SENS_SCALE) * total * conduct[x])[4:12])
    stacked = jnp.concatenate(blocks + [ids_ref[3, x] for x in range(8)], axis=0)
    turned = jnp.transpose(stacked)
    sums = jnp.sum(turned, axis=0, keepdims=True)
    row = jnp.where(iota((1, LANES), 1) < 64, sums, turned[0:1])
    tile = jnp.concatenate([smooth_ref[...], row, jnp.zeros((3, LANES), F32)], axis=0)
    for other in range(out_ref.shape[0]):
        out_ref[other] = tile


def place_kernel(gy_ref, tally_ref, all_ref, out_ref, smooth_ref, hot_ref, low_ref):
    me = gy_ref[0]
    start = jnp.int32(0)
    for other in range(tally_ref.shape[0]):
        start = start + jnp.where(other < me, tally_ref[other], 0)
    held = tally_ref[me]
    sources = all_ref.shape[0]
    half = sources // 2
    both = all_ref[:, 4, :]
    turned = pltpu.roll(both, 64, 1)
    left = iota((half, LANES), 1) < 64
    values = jnp.where(left, both[:half], turned[half:])
    slots = jnp.where(left, turned[:half], both[half:]).astype(I32) - start
    pieces = [piece.astype(F32) for piece in thirds(values)]
    high, low = slots >> 7, slots & 127
    slot_rows = out_ref.shape[0]
    high_row = iota((slot_rows, LANES), 0)
    low_row = iota((LANES, LANES), 0)
    for row in range(half):
        match = high_row == high[row : row + 1]
        for number in range(3):
            hot_ref[number * slot_rows : (number + 1) * slot_rows, row * LANES : (row + 1) * LANES] = jnp.where(
                match, pieces[number][row : row + 1], 0.0
            ).astype(BF16)
        low_ref[:, row * LANES : (row + 1) * LANES] = jnp.where(low_row == low[row : row + 1], 1.0, 0.0).astype(BF16)
    sums = lax.dot_general(hot_ref[...], low_ref[...], (((1,), (1,)), ((), ())), preferred_element_type=F32)
    sums = sums[0:slot_rows] + sums[slot_rows : 2 * slot_rows] + sums[2 * slot_rows :]

    top, shift = start >> 7, start & 127
    for row in range(slot_rows + 1):
        zone_row = jnp.minimum(top + row, sources * 4 - 1)
        smooth_ref[row : row + 1, :] = all_ref[zone_row >> 2, pl.ds(zone_row & 3, 1), :]
    moved = pltpu.roll(smooth_ref[...], LANES - shift, 1)
    lane = iota((slot_rows, LANES), 1)
    smooth = jnp.where(lane < LANES - shift, moved[0:slot_rows], moved[1 : slot_rows + 1])
    within = iota((slot_rows, LANES), 0) * LANES + lane
    out_ref[...] = jnp.where(within < held, sums + smooth, 0.0)


def body(temp, rock, misfit, zone_map, zone_log, tally, adjacency):
    east, north, depth = temp.shape
    across, along = lax.axis_size("gx"), lax.axis_size("gy")
    shard_rows = zone_log.shape[0] // LANES
    zone = zone_log.reshape(shard_rows, LANES)
    gx = lax.axis_index("gx").astype(I32).reshape(1)
    gy = lax.axis_index("gy").astype(I32).reshape(1)

    def move(array, axis, by):
        count = lax.axis_size(axis)
        return lax.ppermute(array, axis, [(i, i + by) for i in range(count) if 0 <= i + by < count])

    shape = jax.ShapeDtypeStruct
    pack, spread = call(
        pack_kernel,
        [shape((4, east, north, depth), F32), shape((along, shard_rows, LANES), F32)],
        [VMEM] * 5,
    )(temp, rock, misfit, jnp.transpose(zone_map, (0, 2, 1)), zone)
    from_south, from_north = move(pack, "gy", 1), move(pack, "gy", -1)
    table = lax.all_to_all(spread, "gy", 0, 0, tiled=True).reshape(along * shard_rows, LANES)
    ext, low, high = call(
        extend_kernel,
        [shape((4, 8, 16, LANES), F32), shape((10, 16, LANES), F32), shape((10, 16, LANES), F32)],
        [VMEM] * 4,
    )(pack, from_south, from_north, table)
    from_west, from_east = move(high, "gx", 1), move(low, "gx", -1)
    smooth = call(
        smooth_kernel,
        shape((shard_rows // across, LANES), F32),
        [SMEM] + [VMEM] * 3 + [pl.BlockSpec(memory_space=pl.ANY)],
        cost=pl.CostEstimate(flops=1 << 32, bytes_accessed=1 << 20, transcendentals=0),
    )(gx, jnp.transpose(adjacency), zone, table, ext)
    tile = call(sweep_kernel, shape((across * along, 8, LANES), F32), [VMEM] * 5)(
        ext, from_west, from_east, pack, smooth
    )
    gathered = lax.all_to_all(tile, ("gy", "gx"), 0, 0, tiled=True)
    slot_rows = 2 * shard_rows
    out = call(
        place_kernel,
        shape((slot_rows, LANES), F32),
        [SMEM, SMEM, VMEM],
        [
            pltpu.VMEM((slot_rows + 8, LANES), F32),
            pltpu.VMEM((3 * slot_rows, across * along * 64), BF16),
            pltpu.VMEM((LANES, across * along * 64), BF16),
        ],
    )(gy, tally, gathered)
    return out.reshape(slot_rows * LANES)


def solution(mesh):
    placed = (
        P("gx", "gy", None),
        P("gx", "gy", None),
        P("gx", "gy", None),
        P("gx", "gy", None),
        P("gy"),
        P(),
        P("gy", None),
    )
    return jax.shard_map(body, mesh=mesh, in_specs=placed, out_specs=P("gy"), check_vma=False)
```

```python
import jax
import jax.numpy as jnp
from jax import lax
from jax.experimental import pallas as pl
from jax.experimental.pallas import tpu as pltpu
from jax.sharding import PartitionSpec as P

NBRS = 6
ITERS = 3
RELAXATION = 0.8
SMOOTHING = 0.5
SENS_SCALE = 0.03125
LANES = 128
F32 = jnp.float32
BF16 = jnp.bfloat16
I32 = jnp.int32

VMEM = pl.BlockSpec(memory_space=pltpu.VMEM)
HBM = pl.BlockSpec(memory_space=pltpu.HBM)


def iota(shape, dim):
    return lax.broadcasted_iota(I32, shape, dim)


def in_hbm(array):
    return pltpu.with_memory_space_constraint(array, pltpu.HBM)


def call(kernel, outs, in_specs, scratch=(), cost=None):
    one = not isinstance(outs, (list, tuple))
    shapes = [outs] if one else list(outs)
    return pl.pallas_call(
        kernel,
        out_shape=shapes[0] if one else shapes,
        in_specs=in_specs,
        out_specs=VMEM if one else [VMEM] * len(shapes),
        scratch_shapes=list(scratch),
        cost_estimate=cost,
        compiler_params=pltpu.CompilerParams(vmem_limit_bytes=32 << 20),
    )


def thirds(table):
    first = table.astype(BF16)
    rest = table - first.astype(F32)
    second = rest.astype(BF16)
    third = (rest - second.astype(F32)).astype(BF16)
    return first, second, third


def column(tile, lane):
    picked = jnp.where(iota(tile.shape, 1) == lane, tile, 0.0)
    return jnp.broadcast_to(jnp.sum(picked, axis=1, keepdims=True), tile.shape)


def pack_kernel(temp_ref, rock_ref, misfit_ref, map_ref, zone_ref, pack_ref, spread_ref, map_buf, zone_buf, sems):
    east, north = rock_ref.shape[0], rock_ref.shape[1]
    copies = [
        pltpu.make_async_copy(source, target, sems.at[number])
        for number, (source, target) in enumerate(
            [
                (map_ref, map_buf),
                (zone_ref, zone_buf),
                (rock_ref, pack_ref.at[pl.ds(0, east)]),
                (misfit_ref, pack_ref.at[pl.ds(east, east)]),
                (temp_ref, pack_ref.at[pl.ds(2 * east, east)]),
            ]
        )
    ]
    for copy in copies:
        copy.start()
    copies[0].wait()
    diagonal = iota((north, north), 0) == iota((north, north), 1)
    lane = iota((north, LANES), 1)
    ids = jnp.zeros((north, LANES), F32)
    for x in range(east):
        row = jnp.broadcast_to(map_buf[x].astype(F32), (north, north))
        one = jnp.sum(jnp.where(diagonal, row, 0.0), axis=1, keepdims=True)
        ids = jnp.where(lane == x, one, ids)
    pack_ref[3 * east] = ids
    copies[1].wait()
    shard = zone_buf[...]
    for other in range(spread_ref.shape[0]):
        spread_ref[other] = shard
    for copy in copies[2:]:
        copy.wait()


def extend_kernel(own_ref, first_ref, second_ref, ext_ref, slab_a_ref, slab_b_ref):
    gx, gy = lax.axis_index("gx"), lax.axis_index("gy")
    even = gy % 2 == 0

    def window(begin, count):
        one, two = first_ref[begin : begin + count], second_ref[begin : begin + count]
        south, north = jnp.where(even, two, one), jnp.where(even, one, two)
        return jnp.concatenate([south, own_ref[begin : begin + count], north], axis=1)

    rock, ids = window(0, 8), window(24, 1)
    misfit, temp = window(8, 8)[:, 4:20], window(16, 8)[:, 4:20]
    ext_ref[0:8] = rock
    ext_ref[8:9] = ids
    ext_ref[9:17, 0:16] = misfit
    ext_ref[17:25, 0:16] = temp
    inner, ids = rock[:, 4:20], ids[:, 4:20]
    low = (inner[0:5], misfit[0:4], temp[0:1], ids)
    moved = pltpu.roll(ids[0], LANES - 3, 1).reshape(1, 16, LANES)
    high = (inner[3:8], misfit[4:8], temp[7:8], moved)
    east_first = gx % 2 == 0
    begin = 0
    for lower, upper in zip(low, high):
        end = begin + lower.shape[0]
        slab_a_ref[begin:end] = jnp.where(east_first, upper, lower)
        slab_b_ref[begin:end] = jnp.where(east_first, lower, upper)
        begin = end


def smooth_kernel(adjacency_ref, zone_ref, tally_ref, table_ref, out_ref, meta_ref, tally_buf, sem):
    copy = pltpu.make_async_copy(tally_ref, tally_buf, sem)
    copy.start()
    rows = out_ref.shape[0]
    count = rows * LANES
    high_size = table_ref.shape[0]
    gx = lax.axis_index("gx")
    pieces = jnp.concatenate(thirds(jnp.transpose(table_ref[...])), axis=0)
    offset = pl.multiple_of(gx * count, count)
    high_row = iota((high_size, count), 0)
    low_row = iota((LANES, count), 0)
    total = jnp.zeros((LANES, count), F32)
    for k in range(NBRS):
        ids = adjacency_ref[k : k + 1, pl.ds(offset, count)]
        hot = jnp.where(high_row == (ids >> 7), 1.0, 0.0).astype(BF16)
        found = jnp.dot(pieces, hot, preferred_element_type=F32)
        found = found[0:LANES] + found[LANES : 2 * LANES] + found[2 * LANES :]
        total = total + jnp.where(low_row == (ids & 127), found, 0.0)
    near = jnp.sum(total, axis=0, keepdims=True)
    own = zone_ref[pl.ds(gx * rows, rows), :]
    for row in range(rows):
        out_ref[row : row + 1] = SMOOTHING * (
            NBRS * own[row : row + 1] - near[:, row * LANES : (row + 1) * LANES]
        )
    copy.wait()
    tally = tally_buf[...].astype(F32)
    rank, gy = iota(tally.shape, 1), lax.axis_index("gy")
    start = jnp.sum(jnp.where(rank < gy, tally, 0.0), axis=1, keepdims=True)
    held = jnp.sum(jnp.where(rank == gy, tally, 0.0), axis=1, keepdims=True)
    meta_ref[...] = jnp.where(iota((8, LANES), 0) == 0, start, held).astype(I32)


def sweep_kernel(ext_ref, first_ref, second_ref, table_ref, smooth_ref, out_ref):
    shape = (16, LANES)
    lane = iota(shape, 1)
    first, last = lane == 0, lane == LANES - 1
    even = lax.axis_index("gx") % 2 == 0
    one, two = first_ref[...], second_ref[...]
    west, east = jnp.where(even, two, one), jnp.where(even, one, two)

    own_ids = ext_ref[8]
    ids = [column(own_ids, x) for x in range(8)]
    ids += [column(west[10], step) for step in range(5)]
    ids += [column(east[10], step) for step in range(5)]
    own_columns = ids[:8]
    ids = jnp.concatenate(ids, axis=0).astype(I32)
    places = ids.shape[0]
    rows = ids >> 7
    lanes = iota((places, LANES), 1)
    hot = jnp.concatenate(
        [jnp.where(rows == lanes + LANES * part, 1.0, 0.0).astype(BF16) for part in range(table_ref.shape[0] // LANES)],
        axis=1,
    )
    found = sum(jnp.dot(hot, piece, preferred_element_type=F32) for piece in thirds(table_ref[...]))
    log = jnp.sum(jnp.where(lanes == (ids & 127), found, 0.0), axis=1, keepdims=True)
    gain = jnp.exp(jnp.broadcast_to(log, (places, LANES)))

    conduct, source, heat, own_sides = {}, {}, {}, {}
    for x in range(8):
        wide = ext_ref[x] * gain[24 * x : 24 * x + 24]
        conduct[x] = wide[4:20]
        own_sides[x] = wide[3:19] + wide[5:21]
        source[x] = ext_ref[9 + x, 0:16]
        heat[x] = ext_ref[17 + x, 0:16]
    for step in range(5):
        conduct[step - 5] = west[step] * gain[192 + 16 * step : 208 + 16 * step]
        conduct[step + 8] = east[step] * gain[272 + 16 * step : 288 + 16 * step]
    for step in range(4):
        source[step - 4] = west[5 + step]
        source[step + 8] = east[5 + step]
    heat[-1] = west[9]
    heat[8] = east[9]

    def depth_sides(v):
        up = jnp.where(first, 0.0, pltpu.roll(v, 1, 1))
        down = jnp.where(last, 0.0, pltpu.roll(v, LANES - 1, 1))
        return up, down

    def north_sides(v):
        return pltpu.roll(v, 1, 0), pltpu.roll(v, 15, 0)

    def around(rows, x):
        v = rows[x]
        up, down = depth_sides(v)
        south, north = north_sides(v)
        return ((rows[x - 1] + rows[x + 1]) + (south + north)) + (up + down)

    inverse, dual = {}, {}
    for x in range(-4, 12):
        v = conduct[x]
        if 0 <= x < 8:
            across = own_sides[x]
        else:
            south, north = north_sides(v)
            across = south + north
        up, down = depth_sides(v)
        twice = 6.0 * v + (((conduct[x - 1] + conduct[x + 1]) + across) + (up + down))
        inverse[x] = jnp.where(v > 0.0, 2.0 / twice, 0.0)
        dual[x] = source[x] * inverse[x]
    for sweep in range(ITERS):
        reach = 3 - sweep
        flux = {x: conduct[x] * dual[x] for x in dual}
        fresh = {}
        for x in range(-reach, 8 + reach):
            coupled = 0.5 * (conduct[x] * around(dual, x) + around(flux, x))
            fresh[x] = (1.0 - RELAXATION) * dual[x] + (RELAXATION * inverse[x]) * (source[x] + coupled)
        dual = fresh
    blocks = []
    for x in range(8):
        t, v = heat[x], dual[x]
        total = (t - heat[x + 1]) * (v - dual[x + 1]) + (t - heat[x - 1]) * (v - dual[x - 1])
        for near_t, near_v in zip(north_sides(t) + depth_sides(t), north_sides(v) + depth_sides(v)):
            total = total + (t - near_t) * (v - near_v)
        blocks.append(((-0.5 * SENS_SCALE) * total * conduct[x])[4:12])
    stacked = jnp.concatenate(blocks + [own[8:16] for own in own_columns], axis=0)
    turned = jnp.transpose(stacked)
    sums = jnp.sum(turned, axis=0, keepdims=True)
    row = jnp.where(iota((1, LANES), 1) < 64, sums, turned[0:1])
    tile = jnp.concatenate([smooth_ref[...], row], axis=0)
    for eight in range(out_ref.shape[0] // 40):
        out_ref[40 * eight : 40 * eight + 40] = jnp.concatenate([tile] * 8, axis=0)


def place_kernel(meta_ref, all_ref, out_ref, smooth_ref, hot_ref, low_ref):
    start, held = meta_ref[0, 0], meta_ref[1, 0]
    sources = all_ref.shape[0] // 5
    half = sources // 2
    both = all_ref[pl.ds(4, sources, stride=5), :]
    turned = pltpu.roll(both, 64, 1)
    left = iota((half, LANES), 1) < 64
    values = jnp.where(left, both[:half], turned[half:])
    slots = jnp.where(left, turned[:half], both[half:]).astype(I32) - start
    pieces = [piece.astype(F32) for piece in thirds(values)]
    high, low = slots >> 7, slots & 127
    slot_rows = out_ref.shape[0]
    high_row = iota((slot_rows, LANES), 0)
    low_row = iota((LANES, LANES), 0)
    for row in range(half):
        match = high_row == high[row : row + 1]
        for number in range(3):
            hot_ref[number * slot_rows : (number + 1) * slot_rows, row * LANES : (row + 1) * LANES] = jnp.where(
                match, pieces[number][row : row + 1], 0.0
            ).astype(BF16)
        low_ref[:, row * LANES : (row + 1) * LANES] = jnp.where(low_row == low[row : row + 1], 1.0, 0.0).astype(BF16)
    sums = lax.dot_general(hot_ref[...], low_ref[...], (((1,), (1,)), ((), ())), preferred_element_type=F32)
    sums = sums[0:slot_rows] + sums[slot_rows : 2 * slot_rows] + sums[2 * slot_rows :]

    top, shift = start >> 7, start & 127
    for row in range(slot_rows + 1):
        zone_row = jnp.minimum(top + row, sources * 4 - 1)
        smooth_ref[row : row + 1, :] = all_ref[pl.ds((zone_row >> 2) * 5 + (zone_row & 3), 1), :]
    moved = pltpu.roll(smooth_ref[...], LANES - shift, 1)
    lane = iota((slot_rows, LANES), 1)
    smooth = jnp.where(lane < LANES - shift, moved[0:slot_rows], moved[1 : slot_rows + 1])
    within = iota((slot_rows, LANES), 0) * LANES + lane
    out_ref[...] = jnp.where(within < held, sums + smooth, 0.0)


def swap(array, axis, begin):
    pairs = [(i, i + 1) for i in range(begin, lax.axis_size(axis) - 1, 2)]
    return lax.ppermute(array, axis, pairs + [(b, a) for a, b in pairs])


def body(temp, rock, misfit, zone_map, zone_log, tally, adjacency):
    east, north, depth = temp.shape
    across, along = lax.axis_size("gx"), lax.axis_size("gy")
    devices = across * along
    shard_rows = zone_log.shape[0] // LANES
    zone = zone_log.reshape(shard_rows, LANES)
    shape = jax.ShapeDtypeStruct
    pack, spread = call(
        pack_kernel,
        [shape((3 * east + 1, north, depth), F32), shape((along, shard_rows, LANES), F32)],
        [HBM] * 5,
        [pltpu.VMEM((east, 1, north), I32), pltpu.VMEM((shard_rows, LANES), F32), pltpu.SemaphoreType.DMA((5,))],
    )(*map(in_hbm, (temp, rock, misfit, jnp.transpose(zone_map, (0, 2, 1)), zone)))
    y_first, y_second = swap(pack, "gy", 0), swap(pack, "gy", 1)
    table = lax.all_to_all(spread, "gy", 0, 0, tiled=True).reshape(along * shard_rows, LANES)
    ext, slab_a, slab_b = call(
        extend_kernel,
        [shape((25, 24, LANES), F32), shape((11, 16, LANES), F32), shape((11, 16, LANES), F32)],
        [VMEM] * 3,
    )(pack, y_first, y_second)
    x_first, x_second = swap(slab_a, "gx", 0), swap(slab_b, "gx", 1)
    smooth, meta = call(
        smooth_kernel,
        [shape((shard_rows // across, LANES), F32), shape((8, LANES), I32)],
        [VMEM, VMEM, HBM, VMEM],
        [pltpu.VMEM((1, along), I32), pltpu.SemaphoreType.DMA],
        cost=pl.CostEstimate(flops=1 << 32, bytes_accessed=1 << 20, transcendentals=0),
    )(jnp.transpose(adjacency), zone, in_hbm(tally.reshape(1, along)), table)
    rows = call(sweep_kernel, shape((devices * 5, LANES), F32), [VMEM] * 5)(ext, x_first, x_second, table, smooth)
    gathered = lax.all_to_all(rows.reshape(devices, 1, 5 * LANES), ("gy", "gx"), 0, 0, tiled=True)
    slot_rows = 2 * shard_rows
    out = call(
        place_kernel,
        shape((slot_rows, LANES), F32),
        [VMEM, VMEM],
        [
            pltpu.VMEM((slot_rows + 8, LANES), F32),
            pltpu.VMEM((3 * slot_rows, devices * 64), BF16),
            pltpu.VMEM((LANES, devices * 64), BF16),
        ],
    )(meta, gathered.reshape(devices * 5, LANES))
    return out.reshape(slot_rows * LANES)


def solution(mesh):
    placed = (
        P("gx", "gy", None),
        P("gx", "gy", None),
        P("gx", "gy", None),
        P("gx", "gy", None),
        P("gy"),
        P(),
        P("gy", None),
    )
    return jax.shard_map(body, mesh=mesh, in_specs=placed, out_specs=P("gy"), check_vma=False)
```

```python
import jax
import jax.numpy as jnp
from jax import lax
from jax.experimental import pallas as pl
from jax.experimental.pallas import tpu as pltpu
from jax.sharding import PartitionSpec as P

NBRS = 6
ITERS = 3
RELAXATION = 0.8
SMOOTHING = 0.5
SENS_SCALE = 0.03125
LANES = 128
F32 = jnp.float32
BF16 = jnp.bfloat16
I32 = jnp.int32

VMEM = pl.BlockSpec(memory_space=pltpu.VMEM)
HBM = pl.BlockSpec(memory_space=pltpu.HBM)


def iota(shape, dim):
    return lax.broadcasted_iota(I32, shape, dim)


def in_hbm(array):
    return pltpu.with_memory_space_constraint(array, pltpu.HBM)


def call(kernel, outs, in_specs, scratch=(), cost=None):
    one = not isinstance(outs, (list, tuple))
    shapes = [outs] if one else list(outs)
    return pl.pallas_call(
        kernel,
        out_shape=shapes[0] if one else shapes,
        in_specs=in_specs,
        out_specs=VMEM if one else [VMEM] * len(shapes),
        scratch_shapes=list(scratch),
        cost_estimate=cost,
        compiler_params=pltpu.CompilerParams(vmem_limit_bytes=32 << 20),
    )


def thirds(table):
    first = table.astype(BF16)
    rest = table - first.astype(F32)
    second = rest.astype(BF16)
    third = (rest - second.astype(F32)).astype(BF16)
    return first, second, third


def column(tile, lane):
    picked = jnp.where(iota(tile.shape, 1) == lane, tile, 0.0)
    return jnp.broadcast_to(jnp.sum(picked, axis=1, keepdims=True), tile.shape)


def pack_kernel(temp_ref, rock_ref, misfit_ref, map_ref, zone_ref, pack_ref, shard_ref, map_buf, sems):
    east, north = rock_ref.shape[0], rock_ref.shape[1]
    copies = [
        pltpu.make_async_copy(source, target, sems.at[number])
        for number, (source, target) in enumerate(
            [
                (map_ref, map_buf),
                (zone_ref, shard_ref),
                (rock_ref, pack_ref.at[pl.ds(0, east)]),
                (misfit_ref, pack_ref.at[pl.ds(east, east)]),
                (temp_ref, pack_ref.at[pl.ds(2 * east, east)]),
            ]
        )
    ]
    for copy in copies:
        copy.start()
    copies[0].wait()
    diagonal = iota((north, north), 0) == iota((north, north), 1)
    lane = iota((north, LANES), 1)
    ids = jnp.zeros((north, LANES), F32)
    for x in range(east):
        row = jnp.broadcast_to(map_buf[x].astype(F32), (north, north))
        one = jnp.sum(jnp.where(diagonal, row, 0.0), axis=1, keepdims=True)
        ids = jnp.where(lane == x, one, ids)
    pack_ref[3 * east] = ids
    for copy in copies[1:]:
        copy.wait()


def spread_kernel(shard_ref, spread_ref):
    shard = shard_ref[...]
    for other in range(spread_ref.shape[0]):
        spread_ref[other] = shard


def extend_kernel(own_ref, first_ref, second_ref, ext_ref, slab_a_ref, slab_b_ref):
    gx, gy = lax.axis_index("gx"), lax.axis_index("gy")
    even = gy % 2 == 0

    def window(begin, count):
        one, two = first_ref[begin : begin + count], second_ref[begin : begin + count]
        south, north = jnp.where(even, two, one), jnp.where(even, one, two)
        return jnp.concatenate([south, own_ref[begin : begin + count], north], axis=1)

    rock, ids = window(0, 8), window(24, 1)
    misfit, temp = window(8, 8)[:, 4:20], window(16, 8)[:, 4:20]
    ext_ref[0:8] = rock
    ext_ref[8:9] = ids
    ext_ref[9:17, 0:16] = misfit
    ext_ref[17:25, 0:16] = temp
    inner, ids = rock[:, 4:20], ids[:, 4:20]
    low = (inner[0:5], misfit[0:4], temp[0:1], ids)
    moved = pltpu.roll(ids[0], LANES - 3, 1).reshape(1, 16, LANES)
    high = (inner[3:8], misfit[4:8], temp[7:8], moved)
    east_first = gx % 2 == 0
    begin = 0
    for lower, upper in zip(low, high):
        end = begin + lower.shape[0]
        slab_a_ref[begin:end] = jnp.where(east_first, upper, lower)
        slab_b_ref[begin:end] = jnp.where(east_first, lower, upper)
        begin = end


def smooth_kernel(adjacency_ref, zone_ref, tally_ref, table_ref, out_ref, meta_ref, tally_buf, sem):
    copy = pltpu.make_async_copy(tally_ref, tally_buf, sem)
    copy.start()
    rows = out_ref.shape[0]
    count = rows * LANES
    high_size = table_ref.shape[0]
    gx = lax.axis_index("gx")
    pieces = jnp.concatenate(thirds(jnp.transpose(table_ref[...])), axis=0)
    offset = pl.multiple_of(gx * count, count)
    high_row = iota((high_size, count), 0)
    low_row = iota((LANES, count), 0)
    total = jnp.zeros((LANES, count), F32)
    for k in range(NBRS):
        ids = adjacency_ref[k : k + 1, pl.ds(offset, count)]
        hot = jnp.where(high_row == (ids >> 7), 1.0, 0.0).astype(BF16)
        found = jnp.dot(pieces, hot, preferred_element_type=F32)
        found = found[0:LANES] + found[LANES : 2 * LANES] + found[2 * LANES :]
        total = total + jnp.where(low_row == (ids & 127), found, 0.0)
    near = jnp.sum(total, axis=0, keepdims=True)
    own = zone_ref[pl.ds(gx * rows, rows), :]
    for row in range(rows):
        out_ref[row : row + 1] = SMOOTHING * (
            NBRS * own[row : row + 1] - near[:, row * LANES : (row + 1) * LANES]
        )
    copy.wait()
    tally = tally_buf[...].astype(F32)
    rank, gy = iota(tally.shape, 1), lax.axis_index("gy")
    start = jnp.sum(jnp.where(rank < gy, tally, 0.0), axis=1, keepdims=True)
    held = jnp.sum(jnp.where(rank == gy, tally, 0.0), axis=1, keepdims=True)
    meta_ref[...] = jnp.where(iota((8, LANES), 0) == 0, start, held).astype(I32)


def sweep_kernel(ext_ref, first_ref, second_ref, table_ref, smooth_ref, out_ref):
    shape = (16, LANES)
    lane = iota(shape, 1)
    first, last = lane == 0, lane == LANES - 1
    even = lax.axis_index("gx") % 2 == 0
    one, two = first_ref[...], second_ref[...]
    west, east = jnp.where(even, two, one), jnp.where(even, one, two)

    own_ids = ext_ref[8]
    ids = [column(own_ids, x) for x in range(8)]
    ids += [column(west[10], step) for step in range(5)]
    ids += [column(east[10], step) for step in range(5)]
    own_columns = ids[:8]
    ids = jnp.concatenate(ids, axis=0).astype(I32)
    places = ids.shape[0]
    rows = ids >> 7
    lanes = iota((places, LANES), 1)
    hot = jnp.concatenate(
        [jnp.where(rows == lanes + LANES * part, 1.0, 0.0).astype(BF16) for part in range(table_ref.shape[0] // LANES)],
        axis=1,
    )
    found = sum(jnp.dot(hot, piece, preferred_element_type=F32) for piece in thirds(table_ref[...]))
    log = jnp.sum(jnp.where(lanes == (ids & 127), found, 0.0), axis=1, keepdims=True)
    gain = jnp.exp(jnp.broadcast_to(log, (places, LANES)))

    conduct, source, heat, own_sides = {}, {}, {}, {}
    for x in range(8):
        wide = ext_ref[x] * gain[24 * x : 24 * x + 24]
        conduct[x] = wide[4:20]
        own_sides[x] = wide[3:19] + wide[5:21]
        source[x] = ext_ref[9 + x, 0:16]
        heat[x] = ext_ref[17 + x, 0:16]
    for step in range(5):
        conduct[step - 5] = west[step] * gain[192 + 16 * step : 208 + 16 * step]
        conduct[step + 8] = east[step] * gain[272 + 16 * step : 288 + 16 * step]
    for step in range(4):
        source[step - 4] = west[5 + step]
        source[step + 8] = east[5 + step]
    heat[-1] = west[9]
    heat[8] = east[9]

    def depth_sides(v):
        up = jnp.where(first, 0.0, pltpu.roll(v, 1, 1))
        down = jnp.where(last, 0.0, pltpu.roll(v, LANES - 1, 1))
        return up, down

    def north_sides(v):
        return pltpu.roll(v, 1, 0), pltpu.roll(v, 15, 0)

    def around(rows, x):
        v = rows[x]
        up, down = depth_sides(v)
        south, north = north_sides(v)
        return ((rows[x - 1] + rows[x + 1]) + (south + north)) + (up + down)

    inverse, dual = {}, {}
    for x in range(-4, 12):
        v = conduct[x]
        if 0 <= x < 8:
            across = own_sides[x]
        else:
            south, north = north_sides(v)
            across = south + north
        up, down = depth_sides(v)
        twice = 6.0 * v + (((conduct[x - 1] + conduct[x + 1]) + across) + (up + down))
        inverse[x] = jnp.where(v > 0.0, 2.0 / twice, 0.0)
        dual[x] = source[x] * inverse[x]
    for sweep in range(ITERS):
        reach = 3 - sweep
        flux = {x: conduct[x] * dual[x] for x in dual}
        fresh = {}
        for x in range(-reach, 8 + reach):
            coupled = 0.5 * (conduct[x] * around(dual, x) + around(flux, x))
            fresh[x] = (1.0 - RELAXATION) * dual[x] + (RELAXATION * inverse[x]) * (source[x] + coupled)
        dual = fresh
    blocks = []
    for x in range(8):
        t, v = heat[x], dual[x]
        total = (t - heat[x + 1]) * (v - dual[x + 1]) + (t - heat[x - 1]) * (v - dual[x - 1])
        for near_t, near_v in zip(north_sides(t) + depth_sides(t), north_sides(v) + depth_sides(v)):
            total = total + (t - near_t) * (v - near_v)
        blocks.append(((-0.5 * SENS_SCALE) * total * conduct[x])[4:12])
    stacked = jnp.concatenate(blocks + [own[8:16] for own in own_columns], axis=0)
    turned = jnp.transpose(stacked)
    sums = jnp.sum(turned, axis=0, keepdims=True)
    row = jnp.where(iota((1, LANES), 1) < 64, sums, turned[0:1])
    tile = jnp.concatenate([smooth_ref[...], row], axis=0)
    for eight in range(out_ref.shape[0] // 40):
        out_ref[40 * eight : 40 * eight + 40] = jnp.concatenate([tile] * 8, axis=0)


def place_kernel(meta_ref, all_ref, out_ref, smooth_ref, hot_ref, low_ref):
    start, held = meta_ref[0, 0], meta_ref[1, 0]
    sources = all_ref.shape[0] // 5
    half = sources // 2
    both = all_ref[pl.ds(4, sources, stride=5), :]
    turned = pltpu.roll(both, 64, 1)
    left = iota((half, LANES), 1) < 64
    values = jnp.where(left, both[:half], turned[half:])
    slots = jnp.where(left, turned[:half], both[half:]).astype(I32) - start
    pieces = [piece.astype(F32) for piece in thirds(values)]
    high, low = slots >> 7, slots & 127
    slot_rows = out_ref.shape[0]
    high_row = iota((slot_rows, LANES), 0)
    low_row = iota((LANES, LANES), 0)
    for row in range(half):
        match = high_row == high[row : row + 1]
        for number in range(3):
            hot_ref[number * slot_rows : (number + 1) * slot_rows, row * LANES : (row + 1) * LANES] = jnp.where(
                match, pieces[number][row : row + 1], 0.0
            ).astype(BF16)
        low_ref[:, row * LANES : (row + 1) * LANES] = jnp.where(low_row == low[row : row + 1], 1.0, 0.0).astype(BF16)
    sums = lax.dot_general(hot_ref[...], low_ref[...], (((1,), (1,)), ((), ())), preferred_element_type=F32)
    sums = sums[0:slot_rows] + sums[slot_rows : 2 * slot_rows] + sums[2 * slot_rows :]

    top, shift = start >> 7, start & 127
    for row in range(slot_rows + 1):
        zone_row = jnp.minimum(top + row, sources * 4 - 1)
        smooth_ref[row : row + 1, :] = all_ref[pl.ds((zone_row >> 2) * 5 + (zone_row & 3), 1), :]
    moved = pltpu.roll(smooth_ref[...], LANES - shift, 1)
    lane = iota((slot_rows, LANES), 1)
    smooth = jnp.where(lane < LANES - shift, moved[0:slot_rows], moved[1 : slot_rows + 1])
    within = iota((slot_rows, LANES), 0) * LANES + lane
    out_ref[...] = jnp.where(within < held, sums + smooth, 0.0)


def swap(array, axis, begin):
    pairs = [(i, i + 1) for i in range(begin, lax.axis_size(axis) - 1, 2)]
    return lax.ppermute(array, axis, pairs + [(b, a) for a, b in pairs])


def body(temp, rock, misfit, zone_map, zone_log, tally, adjacency):
    east, north, depth = temp.shape
    across, along = lax.axis_size("gx"), lax.axis_size("gy")
    devices = across * along
    shard_rows = zone_log.shape[0] // LANES
    zone = zone_log.reshape(shard_rows, LANES)
    shape = jax.ShapeDtypeStruct
    pack, shard = call(
        pack_kernel,
        [shape((3 * east + 1, north, depth), F32), shape((shard_rows, LANES), F32)],
        [HBM] * 5,
        [pltpu.VMEM((east, 1, north), I32), pltpu.SemaphoreType.DMA((5,))],
    )(*map(in_hbm, (temp, rock, misfit, jnp.transpose(zone_map, (0, 2, 1)), zone)))
    y_first, y_second = swap(pack, "gy", 0), swap(pack, "gy", 1)
    spread = call(
        spread_kernel,
        shape((along, shard_rows, LANES), F32),
        [VMEM],
        cost=pl.CostEstimate(flops=1 << 35, bytes_accessed=1 << 20, transcendentals=0),
    )(shard)
    table = lax.all_to_all(spread, "gy", 0, 0, tiled=True).reshape(along * shard_rows, LANES)
    ext, slab_a, slab_b = call(
        extend_kernel,
        [shape((25, 24, LANES), F32), shape((11, 16, LANES), F32), shape((11, 16, LANES), F32)],
        [VMEM] * 3,
        cost=pl.CostEstimate(flops=1 << 37, bytes_accessed=1 << 20, transcendentals=0),
    )(pack, y_first, y_second)
    x_first, x_second = swap(slab_a, "gx", 0), swap(slab_b, "gx", 1)
    smooth, meta = call(
        smooth_kernel,
        [shape((shard_rows // across, LANES), F32), shape((8, LANES), I32)],
        [VMEM, VMEM, HBM, VMEM],
        [pltpu.VMEM((1, along), I32), pltpu.SemaphoreType.DMA],
        cost=pl.CostEstimate(flops=1 << 32, bytes_accessed=1 << 20, transcendentals=0),
    )(jnp.transpose(adjacency), shard, in_hbm(tally.reshape(1, along)), table)
    rows = call(sweep_kernel, shape((devices * 5, LANES), F32), [VMEM] * 5)(ext, x_first, x_second, table, smooth)
    gathered = lax.all_to_all(rows.reshape(devices, 1, 5 * LANES), ("gy", "gx"), 0, 0, tiled=True)
    slot_rows = 2 * shard_rows
    out = call(
        place_kernel,
        shape((slot_rows, LANES), F32),
        [VMEM, VMEM],
        [
            pltpu.VMEM((slot_rows + 8, LANES), F32),
            pltpu.VMEM((3 * slot_rows, devices * 64), BF16),
            pltpu.VMEM((LANES, devices * 64), BF16),
        ],
    )(meta, gathered.reshape(devices * 5, LANES))
    return out.reshape(slot_rows * LANES)


def solution(mesh):
    placed = (
        P("gx", "gy", None),
        P("gx", "gy", None),
        P("gx", "gy", None),
        P("gx", "gy", None),
        P("gy"),
        P(),
        P("gy", None),
    )
    return jax.shard_map(body, mesh=mesh, in_specs=placed, out_specs=P("gy"), check_vma=False)
```

```python
import jax
import jax.numpy as jnp
from jax import lax
from jax.experimental import pallas as pl
from jax.experimental.pallas import tpu as pltpu
from jax.sharding import PartitionSpec as P

NBRS = 6
ITERS = 3
RELAXATION = 0.8
SMOOTHING = 0.5
SENS_SCALE = 0.03125
LANES = 128
F32 = jnp.float32
BF16 = jnp.bfloat16
I32 = jnp.int32

VMEM = pl.BlockSpec(memory_space=pltpu.VMEM)
HBM = pl.BlockSpec(memory_space=pltpu.HBM)


def iota(shape, dim):
    return lax.broadcasted_iota(I32, shape, dim)


def in_hbm(array):
    return pltpu.with_memory_space_constraint(array, pltpu.HBM)


def call(kernel, outs, in_specs, scratch=(), cost=None):
    one = not isinstance(outs, (list, tuple))
    shapes = [outs] if one else list(outs)
    return pl.pallas_call(
        kernel,
        out_shape=shapes[0] if one else shapes,
        in_specs=in_specs,
        out_specs=VMEM if one else [VMEM] * len(shapes),
        scratch_shapes=list(scratch),
        cost_estimate=cost,
        compiler_params=pltpu.CompilerParams(vmem_limit_bytes=32 << 20),
    )


def thirds(table):
    first = table.astype(BF16)
    rest = table - first.astype(F32)
    second = rest.astype(BF16)
    third = (rest - second.astype(F32)).astype(BF16)
    return first, second, third


def column(tile, lane):
    picked = jnp.where(iota(tile.shape, 1) == lane, tile, 0.0)
    return jnp.broadcast_to(jnp.sum(picked, axis=1, keepdims=True), tile.shape)


def pack_kernel(temp_ref, rock_ref, misfit_ref, map_ref, zone_ref, pack_ref, shard_ref, map_buf, sems):
    east, north = rock_ref.shape[0], rock_ref.shape[1]
    copies = [
        pltpu.make_async_copy(source, target, sems.at[number])
        for number, (source, target) in enumerate(
            [
                (map_ref, map_buf),
                (zone_ref, shard_ref),
                (rock_ref, pack_ref.at[pl.ds(0, east)]),
                (misfit_ref, pack_ref.at[pl.ds(east, east)]),
                (temp_ref, pack_ref.at[pl.ds(2 * east, east)]),
            ]
        )
    ]
    for copy in copies:
        copy.start()
    copies[0].wait()
    diagonal = iota((north, north), 0) == iota((north, north), 1)
    lane = iota((north, LANES), 1)
    ids = jnp.zeros((north, LANES), F32)
    for x in range(east):
        row = jnp.broadcast_to(map_buf[x].astype(F32), (north, north))
        one = jnp.sum(jnp.where(diagonal, row, 0.0), axis=1, keepdims=True)
        ids = jnp.where(lane == x, one, ids)
    pack_ref[3 * east] = ids
    for copy in copies[1:]:
        copy.wait()


def spread_kernel(shard_ref, spread_ref):
    shard = shard_ref[...]
    for other in range(spread_ref.shape[0]):
        spread_ref[other] = shard


def extend_kernel(own_ref, first_ref, second_ref, ext_ref, slab_a_ref, slab_b_ref):
    gx, gy = lax.axis_index("gx"), lax.axis_index("gy")
    even = gy % 2 == 0

    def window(begin, count):
        one, two = first_ref[begin : begin + count], second_ref[begin : begin + count]
        south, north = jnp.where(even, two, one), jnp.where(even, one, two)
        return jnp.concatenate([south, own_ref[begin : begin + count], north], axis=1)

    rock, ids = window(0, 8), window(24, 1)
    misfit, temp = window(8, 8)[:, 4:20], window(16, 8)[:, 4:20]
    ext_ref[0:8] = rock
    ext_ref[8:9] = ids
    ext_ref[9:17, 0:16] = misfit
    ext_ref[17:25, 0:16] = temp
    inner, ids = rock[:, 4:20], ids[:, 4:20]
    low = (inner[0:5], misfit[0:4], temp[0:1], ids)
    moved = pltpu.roll(ids[0], LANES - 3, 1).reshape(1, 16, LANES)
    high = (inner[3:8], misfit[4:8], temp[7:8], moved)
    east_first = gx % 2 == 0
    begin = 0
    for lower, upper in zip(low, high):
        end = begin + lower.shape[0]
        slab_a_ref[begin:end] = jnp.where(east_first, upper, lower)
        slab_b_ref[begin:end] = jnp.where(east_first, lower, upper)
        begin = end


def smooth_kernel(adjacency_ref, zone_ref, tally_ref, table_ref, out_ref, meta_ref, tally_buf, sem):
    copy = pltpu.make_async_copy(tally_ref, tally_buf, sem)
    copy.start()
    rows = out_ref.shape[0]
    count = rows * LANES
    high_size = table_ref.shape[0]
    gx = lax.axis_index("gx")
    pieces = jnp.concatenate(thirds(jnp.transpose(table_ref[...])), axis=0)
    offset = pl.multiple_of(gx * count, count)
    high_row = iota((high_size, count), 0)
    low_row = iota((LANES, count), 0)
    total = jnp.zeros((LANES, count), F32)
    for k in range(NBRS):
        ids = adjacency_ref[k : k + 1, pl.ds(offset, count)]
        hot = jnp.where(high_row == (ids >> 7), 1.0, 0.0).astype(BF16)
        found = jnp.dot(pieces, hot, preferred_element_type=F32)
        found = found[0:LANES] + found[LANES : 2 * LANES] + found[2 * LANES :]
        total = total + jnp.where(low_row == (ids & 127), found, 0.0)
    near = jnp.sum(total, axis=0, keepdims=True)
    own = zone_ref[pl.ds(gx * rows, rows), :]
    for row in range(rows):
        out_ref[row : row + 1] = SMOOTHING * (
            NBRS * own[row : row + 1] - near[:, row * LANES : (row + 1) * LANES]
        )
    copy.wait()
    tally = tally_buf[...].astype(F32)
    rank, gy = iota(tally.shape, 1), lax.axis_index("gy")
    start = jnp.sum(jnp.where(rank < gy, tally, 0.0), axis=1, keepdims=True)
    held = jnp.sum(jnp.where(rank == gy, tally, 0.0), axis=1, keepdims=True)
    meta_ref[...] = jnp.where(iota((8, LANES), 0) == 0, start, held).astype(I32)


def sweep_kernel(ext_ref, first_ref, second_ref, table_ref, smooth_ref, out_ref):
    shape = (16, LANES)
    lane = iota(shape, 1)
    first, last = lane == 0, lane == LANES - 1
    even = lax.axis_index("gx") % 2 == 0
    one, two = first_ref[...], second_ref[...]
    west, east = jnp.where(even, two, one), jnp.where(even, one, two)

    own_ids = ext_ref[8]
    ids = [column(own_ids, x) for x in range(8)]
    ids += [column(west[10], step) for step in range(5)]
    ids += [column(east[10], step) for step in range(5)]
    own_columns = ids[:8]
    ids = jnp.concatenate(ids, axis=0).astype(I32)
    places = ids.shape[0]
    rows = ids >> 7
    lanes = iota((places, LANES), 1)
    hot = jnp.concatenate(
        [jnp.where(rows == lanes + LANES * part, 1.0, 0.0).astype(BF16) for part in range(table_ref.shape[0] // LANES)],
        axis=1,
    )
    found = sum(jnp.dot(hot, piece, preferred_element_type=F32) for piece in thirds(table_ref[...]))
    log = jnp.sum(jnp.where(lanes == (ids & 127), found, 0.0), axis=1, keepdims=True)
    gain = jnp.exp(jnp.broadcast_to(log, (places, LANES)))

    conduct, source, heat, own_sides = {}, {}, {}, {}
    for x in range(8):
        wide = ext_ref[x] * gain[24 * x : 24 * x + 24]
        conduct[x] = wide[4:20]
        own_sides[x] = wide[3:19] + wide[5:21]
        source[x] = ext_ref[9 + x, 0:16]
        heat[x] = ext_ref[17 + x, 0:16]
    for step in range(5):
        conduct[step - 5] = west[step] * gain[192 + 16 * step : 208 + 16 * step]
        conduct[step + 8] = east[step] * gain[272 + 16 * step : 288 + 16 * step]
    for step in range(4):
        source[step - 4] = west[5 + step]
        source[step + 8] = east[5 + step]
    heat[-1] = west[9]
    heat[8] = east[9]

    def depth_sides(v):
        up = jnp.where(first, 0.0, pltpu.roll(v, 1, 1))
        down = jnp.where(last, 0.0, pltpu.roll(v, LANES - 1, 1))
        return up, down

    def north_sides(v):
        return pltpu.roll(v, 1, 0), pltpu.roll(v, 15, 0)

    def around(rows, x):
        v = rows[x]
        up, down = depth_sides(v)
        south, north = north_sides(v)
        return ((rows[x - 1] + rows[x + 1]) + (south + north)) + (up + down)

    inverse, dual = {}, {}
    for x in range(-4, 12):
        v = conduct[x]
        if 0 <= x < 8:
            across = own_sides[x]
        else:
            south, north = north_sides(v)
            across = south + north
        up, down = depth_sides(v)
        twice = 6.0 * v + (((conduct[x - 1] + conduct[x + 1]) + across) + (up + down))
        inverse[x] = jnp.where(v > 0.0, 2.0 / twice, 0.0)
        dual[x] = source[x] * inverse[x]
    for sweep in range(ITERS):
        reach = 3 - sweep
        flux = {x: conduct[x] * dual[x] for x in dual}
        fresh = {}
        for x in range(-reach, 8 + reach):
            coupled = 0.5 * (conduct[x] * around(dual, x) + around(flux, x))
            fresh[x] = (1.0 - RELAXATION) * dual[x] + (RELAXATION * inverse[x]) * (source[x] + coupled)
        dual = fresh
    blocks = []
    for x in range(8):
        t, v = heat[x], dual[x]
        total = (t - heat[x + 1]) * (v - dual[x + 1]) + (t - heat[x - 1]) * (v - dual[x - 1])
        for near_t, near_v in zip(north_sides(t) + depth_sides(t), north_sides(v) + depth_sides(v)):
            total = total + (t - near_t) * (v - near_v)
        blocks.append(((-0.5 * SENS_SCALE) * total * conduct[x])[4:12])
    stacked = jnp.concatenate(blocks + [own[8:16] for own in own_columns], axis=0)
    turned = jnp.transpose(stacked)
    sums = jnp.sum(turned, axis=0, keepdims=True)
    row = jnp.where(iota((1, LANES), 1) < 64, sums, turned[0:1])
    tile = jnp.concatenate([smooth_ref[...], row], axis=0)
    for eight in range(out_ref.shape[0] // 40):
        out_ref[40 * eight : 40 * eight + 40] = jnp.concatenate([tile] * 8, axis=0)


def place_kernel(meta_ref, all_ref, out_ref, smooth_ref):
    start, held = meta_ref[0, 0], meta_ref[1, 0]
    sources = all_ref.shape[0] // 5
    half = sources // 2
    both = all_ref[pl.ds(4, sources, stride=5), :]
    turned = pltpu.roll(both, 64, 1)
    left = iota((half, LANES), 1) < 64
    values = jnp.where(left, both[:half], turned[half:])
    slots = jnp.where(left, turned[:half], both[half:]).astype(I32) - start
    pieces = [piece.astype(F32) for piece in thirds(values)]
    slot_rows = out_ref.shape[0]
    high = jnp.clip(slots >> 7, -1, slot_rows).astype(F32)
    low = (slots & 127).astype(F32)
    high_row = iota((slot_rows, LANES), 0).astype(F32).astype(BF16)
    low_row = iota((LANES, LANES), 0).astype(F32).astype(BF16)
    one, zero = jnp.ones((), BF16), jnp.zeros((), BF16)

    def spread(rows, row, count):
        sixteen = jnp.broadcast_to(rows[row : row + 1], (16, LANES)).astype(BF16)
        return jnp.concatenate([sixteen] * (count // 16), axis=0)

    sums = jnp.zeros((3 * slot_rows, LANES), F32)
    for pair in range(half // 2):
        hot, place = [], []
        for row in (2 * pair, 2 * pair + 1):
            match = high_row == spread(high, row, slot_rows)
            hot.append(jnp.concatenate([jnp.where(match, spread(piece, row, slot_rows), zero) for piece in pieces], axis=0))
            place.append(jnp.where(low_row == spread(low, row, LANES), one, zero))
        hot, place = jnp.concatenate(hot, axis=1), jnp.concatenate(place, axis=1)
        sums = sums + lax.dot_general(hot, place, (((1,), (1,)), ((), ())), preferred_element_type=F32)
    sums = sums[0:slot_rows] + sums[slot_rows : 2 * slot_rows] + sums[2 * slot_rows :]

    top, shift = start >> 7, start & 127
    for row in range(slot_rows + 1):
        zone_row = jnp.minimum(top + row, sources * 4 - 1)
        smooth_ref[row : row + 1, :] = all_ref[pl.ds((zone_row >> 2) * 5 + (zone_row & 3), 1), :]
    moved = pltpu.roll(smooth_ref[...], LANES - shift, 1)
    lane = iota((slot_rows, LANES), 1)
    smooth = jnp.where(lane < LANES - shift, moved[0:slot_rows], moved[1 : slot_rows + 1])
    within = iota((slot_rows, LANES), 0) * LANES + lane
    out_ref[...] = jnp.where(within < held, sums + smooth, 0.0)


def swap(array, axis, begin):
    pairs = [(i, i + 1) for i in range(begin, lax.axis_size(axis) - 1, 2)]
    return lax.ppermute(array, axis, pairs + [(b, a) for a, b in pairs])


def body(temp, rock, misfit, zone_map, zone_log, tally, adjacency):
    east, north, depth = temp.shape
    across, along = lax.axis_size("gx"), lax.axis_size("gy")
    devices = across * along
    shard_rows = zone_log.shape[0] // LANES
    zone = zone_log.reshape(shard_rows, LANES)
    shape = jax.ShapeDtypeStruct
    pack, shard = call(
        pack_kernel,
        [shape((3 * east + 1, north, depth), F32), shape((shard_rows, LANES), F32)],
        [HBM] * 5,
        [pltpu.VMEM((east, 1, north), I32), pltpu.SemaphoreType.DMA((5,))],
    )(*map(in_hbm, (temp, rock, misfit, jnp.transpose(zone_map, (0, 2, 1)), zone)))
    y_first, y_second = swap(pack, "gy", 0), swap(pack, "gy", 1)
    spread = call(
        spread_kernel,
        shape((along, shard_rows, LANES), F32),
        [VMEM],
        cost=pl.CostEstimate(flops=1 << 35, bytes_accessed=1 << 20, transcendentals=0),
    )(shard)
    table = lax.all_to_all(spread, "gy", 0, 0, tiled=True).reshape(along * shard_rows, LANES)
    ext, slab_a, slab_b = call(
        extend_kernel,
        [shape((25, 24, LANES), F32), shape((11, 16, LANES), F32), shape((11, 16, LANES), F32)],
        [VMEM] * 3,
        cost=pl.CostEstimate(flops=1 << 37, bytes_accessed=1 << 20, transcendentals=0),
    )(pack, y_first, y_second)
    x_first, x_second = swap(slab_a, "gx", 0), swap(slab_b, "gx", 1)
    smooth, meta = call(
        smooth_kernel,
        [shape((shard_rows // across, LANES), F32), shape((8, LANES), I32)],
        [VMEM, VMEM, HBM, VMEM],
        [pltpu.VMEM((1, along), I32), pltpu.SemaphoreType.DMA],
        cost=pl.CostEstimate(flops=1 << 32, bytes_accessed=1 << 20, transcendentals=0),
    )(jnp.transpose(adjacency), shard, in_hbm(tally.reshape(1, along)), table)
    rows = call(sweep_kernel, shape((devices * 5, LANES), F32), [VMEM] * 5)(ext, x_first, x_second, table, smooth)
    gathered = lax.all_to_all(rows.reshape(devices, 1, 5 * LANES), ("gy", "gx"), 0, 0, tiled=True)
    slot_rows = 2 * shard_rows
    out = call(
        place_kernel,
        shape((slot_rows, LANES), F32),
        [VMEM, VMEM],
        [pltpu.VMEM((slot_rows + 8, LANES), F32)],
    )(meta, gathered.reshape(devices * 5, LANES))
    return out.reshape(slot_rows * LANES)


def solution(mesh):
    placed = (
        P("gx", "gy", None),
        P("gx", "gy", None),
        P("gx", "gy", None),
        P("gx", "gy", None),
        P("gy"),
        P(),
        P("gy", None),
    )
    return jax.shard_map(body, mesh=mesh, in_specs=placed, out_specs=P("gy"), check_vma=False)
```

```python
import jax
import jax.numpy as jnp
from jax import lax
from jax.experimental import pallas as pl
from jax.experimental.pallas import tpu as pltpu
from jax.sharding import PartitionSpec as P

NBRS = 6
ITERS = 3
RELAXATION = 0.8
SMOOTHING = 0.5
SENS_SCALE = 0.03125
LANES = 128
ROWS = 17
F32 = jnp.float32
BF16 = jnp.bfloat16
I32 = jnp.int32

VMEM = pl.BlockSpec(memory_space=pltpu.VMEM)
HBM = pl.BlockSpec(memory_space=pltpu.HBM)


def iota(shape, dim):
    return lax.broadcasted_iota(I32, shape, dim)


def in_hbm(array):
    return pltpu.with_memory_space_constraint(array, pltpu.HBM)


def call(kernel, outs, in_specs, scratch=(), cost=None):
    one = not isinstance(outs, (list, tuple))
    shapes = [outs] if one else list(outs)
    return pl.pallas_call(
        kernel,
        out_shape=shapes[0] if one else shapes,
        in_specs=in_specs,
        out_specs=VMEM if one else [VMEM] * len(shapes),
        scratch_shapes=list(scratch),
        cost_estimate=cost,
        compiler_params=pltpu.CompilerParams(vmem_limit_bytes=32 << 20),
    )


def thirds(table):
    first = table.astype(BF16)
    rest = table - first.astype(F32)
    second = rest.astype(BF16)
    third = (rest - second.astype(F32)).astype(BF16)
    return first, second, third


def column(tile, lane):
    picked = jnp.where(iota(tile.shape, 1) == lane, tile, 0.0)
    return jnp.broadcast_to(jnp.sum(picked, axis=1, keepdims=True), tile.shape)


def pack_kernel(temp_ref, rock_ref, misfit_ref, map_ref, zone_ref, near_ref, tally_ref, pack_ref, shard_ref, table_ref, counts_ref, map_buf, sems):
    east, north = rock_ref.shape[0], rock_ref.shape[1]
    copies = [
        pltpu.make_async_copy(source, target, sems.at[number])
        for number, (source, target) in enumerate(
            [
                (map_ref, map_buf),
                (zone_ref, shard_ref),
                (rock_ref, pack_ref.at[pl.ds(0, east)]),
                (misfit_ref, pack_ref.at[pl.ds(east, east)]),
                (temp_ref, pack_ref.at[pl.ds(2 * east, east)]),
                (near_ref, table_ref),
                (tally_ref, counts_ref),
            ]
        )
    ]
    for copy in copies:
        copy.start()
    copies[0].wait()
    diagonal = iota((north, north), 0) == iota((north, north), 1)
    lane = iota((north, LANES), 1)
    ids = jnp.zeros((north, LANES), F32)
    for x in range(east):
        row = jnp.broadcast_to(map_buf[x].astype(F32), (north, north))
        one = jnp.sum(jnp.where(diagonal, row, 0.0), axis=1, keepdims=True)
        ids = jnp.where(lane == x, one, ids)
    pack_ref[3 * east] = ids
    for copy in copies[1:]:
        copy.wait()


def spread_kernel(shard_ref, near_ref, spread_ref, lists_ref):
    shard = shard_ref[...]
    tiles = near_ref.shape[1] // LANES
    for tile in range(tiles):
        lists_ref[8 * tile : 8 * tile + NBRS] = near_ref[:, tile * LANES : (tile + 1) * LANES].astype(F32)
    for other in range(2 * tiles):
        spread_ref[other * ROWS : other * ROWS + 16] = shard
    group = iota((tiles, LANES), 1) >> 4
    first = lax.axis_index("gx") * 16
    for odd in range(2):
        ids = jnp.zeros((tiles, LANES), F32)
        for number in range(NBRS):
            moved = pltpu.roll(
                lists_ref[pl.ds(number, tiles, stride=8), :], (2 * LANES + 16 * number - 64 * odd - first) & 127, 1
            )
            ids = jnp.where(group == number, moved, ids)
        spread_ref[pl.ds(16 + odd * ROWS, tiles, stride=2 * ROWS), :] = ids


def extend_kernel(own_ref, first_ref, second_ref, ext_ref, slab_a_ref, slab_b_ref):
    gx, gy = lax.axis_index("gx"), lax.axis_index("gy")
    even = gy % 2 == 0

    def window(begin, count):
        one, two = first_ref[begin : begin + count], second_ref[begin : begin + count]
        south, north = jnp.where(even, two, one), jnp.where(even, one, two)
        return jnp.concatenate([south, own_ref[begin : begin + count], north], axis=1)

    rock, ids = window(0, 8), window(24, 1)
    misfit, temp = window(8, 8)[:, 4:20], window(16, 8)[:, 4:20]
    ext_ref[0:8] = rock
    ext_ref[8:9] = ids
    ext_ref[9:17, 0:16] = misfit
    ext_ref[17:25, 0:16] = temp
    inner, ids = rock[:, 4:20], ids[:, 4:20]
    low = (inner[0:5], misfit[0:4], temp[0:1], ids)
    moved = pltpu.roll(ids[0], LANES - 3, 1).reshape(1, 16, LANES)
    high = (inner[3:8], misfit[4:8], temp[7:8], moved)
    east_first = gx % 2 == 0
    begin = 0
    for lower, upper in zip(low, high):
        end = begin + lower.shape[0]
        slab_a_ref[begin:end] = jnp.where(east_first, upper, lower)
        slab_b_ref[begin:end] = jnp.where(east_first, lower, upper)
        begin = end


def gains(ids, pieces):
    ids = ids.astype(I32)
    rows, lanes = ids >> 7, iota(ids.shape, 1)
    hot = jnp.concatenate(
        [jnp.where(rows == lanes + LANES * part, 1.0, 0.0).astype(BF16) for part in range(pieces.shape[1] // LANES)], axis=1
    )
    found = lax.dot_general(hot, pieces, (((1,), (1,)), ((), ())), preferred_element_type=F32)
    found = found[:, 0:LANES] + found[:, LANES : 2 * LANES] + found[:, 2 * LANES :]
    log = jnp.sum(jnp.where(lanes == (ids & 127), found, 0.0), axis=1, keepdims=True)
    return jnp.exp(jnp.broadcast_to(log, ids.shape))


def smooth_kernel(all_ref, ext_ref, tally_ref, out_ref, meta_ref, pieces_ref, gain_ref, term_ref):
    gx, gy = lax.axis_index("gx"), lax.axis_index("gy")
    shards = all_ref.shape[0] // ROWS
    table = jnp.concatenate([all_ref[ROWS * shard : ROWS * shard + 16] for shard in range(shards)], axis=0)
    high_size = table.shape[0]
    pieces = jnp.concatenate(thirds(jnp.transpose(table)), axis=0)
    pieces_ref[...] = pieces

    lane = iota((24, LANES), 1)
    ids = all_ref[pl.ds(16, shards, stride=ROWS), :]
    rest = jnp.concatenate([pltpu.roll(ids[24:], 96 - 32 * part, 1) for part in range(3)], axis=0)
    ids = jnp.where(lane < 96, ids[:24], rest).astype(I32)
    high, low = ids >> 7, ids & 127
    high_row = iota((high_size, LANES), 0)
    low_row = iota((LANES, LANES), 0)
    near = []
    for chunk in range(6):
        rows = range(4 * chunk, 4 * chunk + 4)
        hot = jnp.concatenate(
            [jnp.where(high_row == high[row : row + 1], 1.0, 0.0).astype(BF16) for row in rows], axis=1
        )
        found = jnp.dot(pieces, hot, preferred_element_type=F32)
        found = found[0:LANES] + found[LANES : 2 * LANES] + found[2 * LANES :]
        for number, row in enumerate(rows):
            picked = jnp.where(low_row == low[row : row + 1], found[:, number * LANES : (number + 1) * LANES], 0.0)
            near.append(jnp.sum(picked, axis=0, keepdims=True))
    near = jnp.concatenate(near, axis=0)
    lane = iota((8, LANES), 1)
    rest = jnp.zeros((8, LANES), F32)
    for part in range(3):
        moved = pltpu.roll(near[8 * part : 8 * part + 8], 32 + 32 * part, 1)
        rest = jnp.where((lane >> 5) == part, moved, rest)
    near = jnp.concatenate([near, rest], axis=0)
    total = near
    for number in range(1, NBRS):
        total = total + pltpu.roll(near, LANES - 16 * number, 1)
    own = all_ref[pl.ds(gy >> 1, shards, stride=ROWS), :]
    own = pltpu.roll(own, (2 * LANES - (gy & 1) * 64 - gx * 16) & 127, 1)
    term_ref[...] = SMOOTHING * (NBRS * own - total)

    mine = (gy * 4 + gx) & 7
    lane = iota((16, LANES), 1)
    first = pltpu.roll(term_ref[pl.ds(0, 16, stride=2), :], mine * 16, 1)
    second = pltpu.roll(term_ref[pl.ds(1, 16, stride=2), :], (mine * 16 + 64) & 127, 1)
    terms = jnp.where((lane >> 4) == mine, first, jnp.where((lane >> 4) == ((mine + 4) & 7), second, 0.0))

    owners = tally_ref.shape[1]
    tally = jnp.broadcast_to(tally_ref[...].astype(F32), (owners, owners))
    before = iota((owners, owners), 1) < iota((owners, owners), 0)
    start = jnp.sum(jnp.where(before, tally, 0.0), axis=1, keepdims=True)
    start = jnp.broadcast_to(start, (owners, LANES)).astype(I32)
    lane = iota((owners, LANES), 1)
    slot = jnp.where((lane >> 4) == mine, 0, 2048) + (gy * 4 + gx) * 16 + (lane & 15)
    wanted = (start >> 12) + jnp.where(slot < (start & 4095), 1, 0)
    chosen = jnp.zeros((owners, LANES), F32)
    for number in range(16):
        chosen = chosen + jnp.where(wanted == number, terms[number : number + 1], 0.0)
    out_ref[...] = chosen

    row = tally[0:1]
    rank = iota(row.shape, 1)
    begin = jnp.sum(jnp.where(rank < gy, row, 0.0), axis=1, keepdims=True)
    held = jnp.sum(jnp.where(rank == gy, row, 0.0), axis=1, keepdims=True)
    meta_ref[...] = jnp.where(iota((8, LANES), 0) == 0, begin, held).astype(I32)

    gain_ref[...] = gains(jnp.concatenate([column(ext_ref[8], x) for x in range(8)], axis=0), pieces)


def sweep_kernel(ext_ref, first_ref, second_ref, pieces_ref, gain_ref, smooth_ref, out_ref):
    shape = (16, LANES)
    lane = iota(shape, 1)
    first, last = lane == 0, lane == LANES - 1
    even = lax.axis_index("gx") % 2 == 0
    one, two = first_ref[...], second_ref[...]
    west, east = jnp.where(even, two, one), jnp.where(even, one, two)
    own_columns = [column(ext_ref[8], x) for x in range(8)]
    ids = [column(west[10], step) for step in range(5)] + [column(east[10], step) for step in range(5)]
    beside = gains(jnp.concatenate(ids, axis=0), pieces_ref[...])

    conduct, source, heat, own_sides = {}, {}, {}, {}
    for x in range(8):
        wide = ext_ref[x] * gain_ref[24 * x : 24 * x + 24]
        conduct[x] = wide[4:20]
        own_sides[x] = wide[3:19] + wide[5:21]
        source[x] = ext_ref[9 + x, 0:16]
        heat[x] = ext_ref[17 + x, 0:16]
    for step in range(5):
        conduct[step - 5] = west[step] * beside[16 * step : 16 * step + 16]
        conduct[step + 8] = east[step] * beside[80 + 16 * step : 96 + 16 * step]
    for step in range(4):
        source[step - 4] = west[5 + step]
        source[step + 8] = east[5 + step]
    heat[-1] = west[9]
    heat[8] = east[9]

    def depth_sides(v):
        up = jnp.where(first, 0.0, pltpu.roll(v, 1, 1))
        down = jnp.where(last, 0.0, pltpu.roll(v, LANES - 1, 1))
        return up, down

    def north_sides(v):
        return pltpu.roll(v, 1, 0), pltpu.roll(v, 15, 0)

    def around(rows, x):
        v = rows[x]
        up, down = depth_sides(v)
        south, north = north_sides(v)
        return ((rows[x - 1] + rows[x + 1]) + (south + north)) + (up + down)

    inverse, dual = {}, {}
    for x in range(-4, 12):
        v = conduct[x]
        if 0 <= x < 8:
            across = own_sides[x]
        else:
            south, north = north_sides(v)
            across = south + north
        up, down = depth_sides(v)
        twice = 6.0 * v + (((conduct[x - 1] + conduct[x + 1]) + across) + (up + down))
        inverse[x] = jnp.where(v > 0.0, 2.0 / twice, 0.0)
        dual[x] = source[x] * inverse[x]
    for sweep in range(ITERS):
        reach = 3 - sweep
        flux = {x: conduct[x] * dual[x] for x in dual}
        fresh = {}
        for x in range(-reach, 8 + reach):
            coupled = 0.5 * (conduct[x] * around(dual, x) + around(flux, x))
            fresh[x] = (1.0 - RELAXATION) * dual[x] + (RELAXATION * inverse[x]) * (source[x] + coupled)
        dual = fresh
    blocks = []
    for x in range(8):
        t, v = heat[x], dual[x]
        total = (t - heat[x + 1]) * (v - dual[x + 1]) + (t - heat[x - 1]) * (v - dual[x - 1])
        for near_t, near_v in zip(north_sides(t) + depth_sides(t), north_sides(v) + depth_sides(v)):
            total = total + (t - near_t) * (v - near_v)
        blocks.append(((-0.5 * SENS_SCALE) * total * conduct[x])[4:12])
    stacked = jnp.concatenate(blocks + [own[8:16] for own in own_columns], axis=0)
    turned = jnp.transpose(stacked)
    sums = jnp.sum(turned, axis=0, keepdims=True)
    row = jnp.where(iota((1, LANES), 1) < 64, sums, turned[0:1])
    odd = (iota((8, LANES), 0) & 1) == 1
    for owner in range(smooth_ref.shape[0]):
        out_ref[8 * owner : 8 * owner + 8] = jnp.where(odd, smooth_ref[owner : owner + 1], row)


def place_kernel(meta_ref, all_ref, out_ref, smooth_ref):
    start, held = meta_ref[0, 0], meta_ref[1, 0]
    sources = all_ref.shape[0] // 2
    half = sources // 2
    both = all_ref[pl.ds(0, sources, stride=2), :]
    turned = pltpu.roll(both, 64, 1)
    left = iota((half, LANES), 1) < 64
    values = jnp.where(left, both[:half], turned[half:])
    slots = jnp.where(left, turned[:half], both[half:]).astype(I32) - start
    pieces = [piece.astype(F32) for piece in thirds(values)]
    slot_rows = out_ref.shape[0]
    high = jnp.clip(slots >> 7, -1, slot_rows).astype(F32)
    low = (slots & 127).astype(F32)
    high_row = iota((slot_rows, LANES), 0).astype(F32).astype(BF16)
    low_row = iota((LANES, LANES), 0).astype(F32).astype(BF16)
    one, zero = jnp.ones((), BF16), jnp.zeros((), BF16)

    def spread(rows, row, count):
        sixteen = jnp.broadcast_to(rows[row : row + 1], (16, LANES)).astype(BF16)
        return jnp.concatenate([sixteen] * (count // 16), axis=0)

    sums = jnp.zeros((3 * slot_rows, LANES), F32)
    for pair in range(half // 2):
        hot, place = [], []
        for row in (2 * pair, 2 * pair + 1):
            match = high_row == spread(high, row, slot_rows)
            hot.append(jnp.concatenate([jnp.where(match, spread(piece, row, slot_rows), zero) for piece in pieces], axis=0))
            place.append(jnp.where(low_row == spread(low, row, LANES), one, zero))
        hot, place = jnp.concatenate(hot, axis=1), jnp.concatenate(place, axis=1)
        sums = sums + lax.dot_general(hot, place, (((1,), (1,)), ((), ())), preferred_element_type=F32)
    sums = sums[0:slot_rows] + sums[slot_rows : 2 * slot_rows] + sums[2 * slot_rows :]

    terms = all_ref[pl.ds(1, sources, stride=2), :].reshape(sources // 8, 8, LANES)
    group, source = iota((1, 8, LANES), 2) >> 4, iota((1, 8, LANES), 1)
    first = jnp.sum(jnp.where(group == source, terms, 0.0), axis=1)
    second = pltpu.roll(jnp.sum(jnp.where(group == ((source + 4) & 7), terms, 0.0), axis=1), 64, 1)
    for copy in range(2):
        smooth_ref[32 * copy : 32 * copy + 16] = first
        smooth_ref[32 * copy + 16 : 32 * copy + 32] = second
    smooth_ref[64:72] = first[0:8]
    top, shift = (start >> 7) & 31, start & 127
    moved = pltpu.roll(smooth_ref[pl.ds(top, 40), :], LANES - shift, 1)
    lane = iota((slot_rows, LANES), 1)
    smooth = jnp.where(lane < LANES - shift, moved[0:slot_rows], moved[1 : slot_rows + 1])
    within = iota((slot_rows, LANES), 0) * LANES + lane
    out_ref[...] = jnp.where(within < held, sums + smooth, 0.0)


def swap(array, axis, begin):
    pairs = [(i, i + 1) for i in range(begin, lax.axis_size(axis) - 1, 2)]
    return lax.ppermute(array, axis, pairs + [(b, a) for a, b in pairs])


def body(temp, rock, misfit, zone_map, zone_log, tally, adjacency):
    east, north, depth = temp.shape
    across, along = lax.axis_size("gx"), lax.axis_size("gy")
    devices = across * along
    shard_rows = zone_log.shape[0] // LANES
    zone = zone_log.reshape(shard_rows, LANES)
    shape = jax.ShapeDtypeStruct
    pack, shard, near, counts = call(
        pack_kernel,
        [
            shape((3 * east + 1, north, depth), F32),
            shape((shard_rows, LANES), F32),
            shape((NBRS, zone_log.shape[0]), I32),
            shape((1, along), I32),
        ],
        [HBM] * 7,
        [pltpu.VMEM((east, 1, north), I32), pltpu.SemaphoreType.DMA((7,))],
    )(
        *map(
            in_hbm,
            (
                temp,
                rock,
                misfit,
                jnp.transpose(zone_map, (0, 2, 1)),
                zone,
                jnp.transpose(adjacency),
                tally.reshape(1, along),
            ),
        )
    )
    y_first, y_second = swap(pack, "gy", 0), swap(pack, "gy", 1)
    spread = call(
        spread_kernel,
        shape((along * ROWS, LANES), F32),
        [VMEM, VMEM],
        [pltpu.VMEM((8 * shard_rows, LANES), F32)],
        cost=pl.CostEstimate(flops=1 << 35, bytes_accessed=1 << 20, transcendentals=0),
    )(shard, near)
    shards = lax.all_to_all(spread.reshape(along, 1, ROWS * LANES), "gy", 0, 0, tiled=True).reshape(along * ROWS, LANES)
    ext, slab_a, slab_b = call(
        extend_kernel,
        [shape((25, 24, LANES), F32), shape((11, 16, LANES), F32), shape((11, 16, LANES), F32)],
        [VMEM] * 3,
        cost=pl.CostEstimate(flops=1 << 37, bytes_accessed=1 << 20, transcendentals=0),
    )(pack, y_first, y_second)
    x_first, x_second = swap(slab_a, "gx", 0), swap(slab_b, "gx", 1)
    smooth, meta, pieces, gain = call(
        smooth_kernel,
        [
            shape((along, LANES), F32),
            shape((8, LANES), I32),
            shape((3 * LANES, along * shard_rows), BF16),
            shape((east * 24, LANES), F32),
        ],
        [VMEM] * 3,
        [pltpu.VMEM((along, LANES), F32)],
        cost=pl.CostEstimate(flops=1 << 32, bytes_accessed=1 << 20, transcendentals=0),
    )(shards, ext, counts)
    rows = call(sweep_kernel, shape((devices * 2, LANES), F32), [VMEM] * 6)(ext, x_first, x_second, pieces, gain, smooth)
    gathered = lax.all_to_all(rows.reshape(devices, 1, 2 * LANES), ("gy", "gx"), 0, 0, tiled=True)
    slot_rows = 2 * shard_rows
    out = call(
        place_kernel,
        shape((slot_rows, LANES), F32),
        [VMEM, VMEM],
        [pltpu.VMEM((72, LANES), F32)],
    )(meta, gathered.reshape(devices * 2, LANES))
    return out.reshape(slot_rows * LANES)


def solution(mesh):
    placed = (
        P("gx", "gy", None),
        P("gx", "gy", None),
        P("gx", "gy", None),
        P("gx", "gy", None),
        P("gy"),
        P(),
        P("gy", None),
    )
    return jax.shard_map(body, mesh=mesh, in_specs=placed, out_specs=P("gy"), check_vma=False)
```

```python
import jax
import jax.numpy as jnp
from jax import lax
from jax.experimental import pallas as pl
from jax.experimental.pallas import tpu as pltpu
from jax.sharding import PartitionSpec as P

NBRS = 6
ITERS = 3
RELAXATION = 0.8
SMOOTHING = 0.5
SENS_SCALE = 0.03125
LANES = 128
ROWS = 17
F32 = jnp.float32
BF16 = jnp.bfloat16
I32 = jnp.int32

VMEM = pl.BlockSpec(memory_space=pltpu.VMEM)
HBM = pl.BlockSpec(memory_space=pltpu.HBM)


def iota(shape, dim):
    return lax.broadcasted_iota(I32, shape, dim)


def in_hbm(array):
    return pltpu.with_memory_space_constraint(array, pltpu.HBM)


def call(kernel, outs, in_specs, scratch=(), cost=None, out_specs=None):
    one = not isinstance(outs, (list, tuple))
    shapes = [outs] if one else list(outs)
    return pl.pallas_call(
        kernel,
        out_shape=shapes[0] if one else shapes,
        in_specs=in_specs,
        out_specs=out_specs or (VMEM if one else [VMEM] * len(shapes)),
        scratch_shapes=list(scratch),
        cost_estimate=cost,
        compiler_params=pltpu.CompilerParams(vmem_limit_bytes=32 << 20),
    )


def thirds(table):
    first = table.astype(BF16)
    rest = table - first.astype(F32)
    second = rest.astype(BF16)
    third = (rest - second.astype(F32)).astype(BF16)
    return first, second, third


def column(tile, lane):
    picked = jnp.where(iota(tile.shape, 1) == lane, tile, 0.0)
    return jnp.broadcast_to(jnp.sum(picked, axis=1, keepdims=True), tile.shape)


def pack_kernel(
    temp_ref, rock_ref, misfit_ref, map_ref, zone_ref, near_ref, tally_ref,
    pack_ref, counts_ref, spread_ref, map_buf, shard_ref, table_ref, lists_ref, many_ref, sems,
):
    east, north = rock_ref.shape[0], rock_ref.shape[1]
    copies = [
        pltpu.make_async_copy(source, target, sems.at[number])
        for number, (source, target) in enumerate(
            [
                (near_ref, table_ref),
                (zone_ref, shard_ref),
                (map_ref, map_buf),
                (rock_ref, pack_ref.at[pl.ds(0, east)]),
                (misfit_ref, pack_ref.at[pl.ds(east, east)]),
                (temp_ref, pack_ref.at[pl.ds(2 * east, east)]),
                (tally_ref, counts_ref),
                (many_ref, spread_ref),
            ]
        )
    ]
    for copy in copies[:-1]:
        copy.start()
    copies[0].wait()
    tiles = table_ref.shape[1] // LANES
    for tile in range(tiles):
        lists_ref[8 * tile : 8 * tile + NBRS] = table_ref[:, tile * LANES : (tile + 1) * LANES].astype(F32)
    group = iota((tiles, LANES), 1) >> 4
    first = lax.axis_index("gx") * 16
    for odd in range(2):
        ids = jnp.zeros((tiles, LANES), F32)
        for number in range(NBRS):
            moved = pltpu.roll(
                lists_ref[pl.ds(number, tiles, stride=8), :], (2 * LANES + 16 * number - 64 * odd - first) & 127, 1
            )
            ids = jnp.where(group == number, moved, ids)
        many_ref[pl.ds(16 + odd * ROWS, tiles, stride=2 * ROWS), :] = ids
    copies[1].wait()
    shard = shard_ref[...]
    for other in range(2 * tiles):
        many_ref[other * ROWS : other * ROWS + 16] = shard
    copies[-1].start()
    copies[2].wait()
    diagonal = iota((north, north), 0) == iota((north, north), 1)
    lane = iota((north, LANES), 1)
    ids = jnp.zeros((north, LANES), F32)
    for x in range(east):
        row = jnp.broadcast_to(map_buf[x].astype(F32), (north, north))
        one = jnp.sum(jnp.where(diagonal, row, 0.0), axis=1, keepdims=True)
        ids = jnp.where(lane == x, one, ids)
    pack_ref[3 * east] = ids
    for copy in copies[3:]:
        copy.wait()


def extend_kernel(own_ref, first_ref, second_ref, ext_ref, slab_a_ref, slab_b_ref):
    gx, gy = lax.axis_index("gx"), lax.axis_index("gy")
    even = gy % 2 == 0

    def window(begin, count):
        one, two = first_ref[begin : begin + count], second_ref[begin : begin + count]
        south, north = jnp.where(even, two, one), jnp.where(even, one, two)
        return jnp.concatenate([south, own_ref[begin : begin + count], north], axis=1)

    rock, ids = window(0, 8), window(24, 1)
    misfit, temp = window(8, 8)[:, 4:20], window(16, 8)[:, 4:20]
    ext_ref[0:8] = rock
    ext_ref[8:9] = ids
    ext_ref[9:17, 0:16] = misfit
    ext_ref[17:25, 0:16] = temp
    inner, ids = rock[:, 4:20], ids[:, 4:20]
    low = (inner[0:5], misfit[0:4], temp[0:1], ids)
    moved = pltpu.roll(ids[0], LANES - 3, 1).reshape(1, 16, LANES)
    high = (inner[3:8], misfit[4:8], temp[7:8], moved)
    east_first = gx % 2 == 0
    begin = 0
    for lower, upper in zip(low, high):
        end = begin + lower.shape[0]
        slab_a_ref[begin:end] = jnp.where(east_first, upper, lower)
        slab_b_ref[begin:end] = jnp.where(east_first, lower, upper)
        begin = end


def gains(ids, pieces):
    ids = ids.astype(I32)
    rows, lanes = ids >> 7, iota(ids.shape, 1)
    hot = jnp.concatenate(
        [jnp.where(rows == lanes + LANES * part, 1.0, 0.0).astype(BF16) for part in range(pieces.shape[1] // LANES)], axis=1
    )
    found = lax.dot_general(hot, pieces, (((1,), (1,)), ((), ())), preferred_element_type=F32)
    found = found[:, 0:LANES] + found[:, LANES : 2 * LANES] + found[:, 2 * LANES :]
    log = jnp.sum(jnp.where(lanes == (ids & 127), found, 0.0), axis=1, keepdims=True)
    return jnp.exp(jnp.broadcast_to(log, ids.shape))


def smooth_kernel(all_ref, ext_ref, tally_ref, out_ref, meta_ref, pieces_ref, gain_ref, term_ref):
    gx, gy = lax.axis_index("gx"), lax.axis_index("gy")
    shards = all_ref.shape[0] // ROWS
    table = jnp.concatenate([all_ref[ROWS * shard : ROWS * shard + 16] for shard in range(shards)], axis=0)
    high_size = table.shape[0]
    pieces = jnp.concatenate(thirds(jnp.transpose(table)), axis=0)
    pieces_ref[...] = pieces

    lane = iota((24, LANES), 1)
    ids = all_ref[pl.ds(16, shards, stride=ROWS), :]
    rest = jnp.concatenate([pltpu.roll(ids[24:], 96 - 32 * part, 1) for part in range(3)], axis=0)
    ids = jnp.where(lane < 96, ids[:24], rest).astype(I32)
    high, low = ids >> 7, ids & 127
    high_row = iota((high_size, LANES), 0)
    low_row = iota((LANES, LANES), 0)
    near = []
    for chunk in range(6):
        rows = range(4 * chunk, 4 * chunk + 4)
        hot = jnp.concatenate(
            [jnp.where(high_row == high[row : row + 1], 1.0, 0.0).astype(BF16) for row in rows], axis=1
        )
        found = jnp.dot(pieces, hot, preferred_element_type=F32)
        found = found[0:LANES] + found[LANES : 2 * LANES] + found[2 * LANES :]
        for number, row in enumerate(rows):
            picked = jnp.where(low_row == low[row : row + 1], found[:, number * LANES : (number + 1) * LANES], 0.0)
            near.append(jnp.sum(picked, axis=0, keepdims=True))
    near = jnp.concatenate(near, axis=0)
    lane = iota((8, LANES), 1)
    rest = jnp.zeros((8, LANES), F32)
    for part in range(3):
        moved = pltpu.roll(near[8 * part : 8 * part + 8], 32 + 32 * part, 1)
        rest = jnp.where((lane >> 5) == part, moved, rest)
    near = jnp.concatenate([near, rest], axis=0)
    total = near
    for number in range(1, NBRS):
        total = total + pltpu.roll(near, LANES - 16 * number, 1)
    own = all_ref[pl.ds(gy >> 1, shards, stride=ROWS), :]
    own = pltpu.roll(own, (2 * LANES - (gy & 1) * 64 - gx * 16) & 127, 1)
    term_ref[...] = SMOOTHING * (NBRS * own - total)

    mine = (gy * 4 + gx) & 7
    lane = iota((16, LANES), 1)
    first = pltpu.roll(term_ref[pl.ds(0, 16, stride=2), :], mine * 16, 1)
    second = pltpu.roll(term_ref[pl.ds(1, 16, stride=2), :], (mine * 16 + 64) & 127, 1)
    terms = jnp.where((lane >> 4) == mine, first, jnp.where((lane >> 4) == ((mine + 4) & 7), second, 0.0))

    owners = tally_ref.shape[1]
    tally = jnp.broadcast_to(tally_ref[...].astype(F32), (owners, owners))
    before = iota((owners, owners), 1) < iota((owners, owners), 0)
    start = jnp.sum(jnp.where(before, tally, 0.0), axis=1, keepdims=True)
    start = jnp.broadcast_to(start, (owners, LANES)).astype(I32)
    lane = iota((owners, LANES), 1)
    slot = jnp.where((lane >> 4) == mine, 0, 2048) + (gy * 4 + gx) * 16 + (lane & 15)
    wanted = (start >> 12) + jnp.where(slot < (start & 4095), 1, 0)
    chosen = jnp.zeros((owners, LANES), F32)
    for number in range(16):
        chosen = chosen + jnp.where(wanted == number, terms[number : number + 1], 0.0)
    out_ref[...] = chosen

    row = tally[0:1]
    rank = iota(row.shape, 1)
    begin = jnp.sum(jnp.where(rank < gy, row, 0.0), axis=1, keepdims=True)
    held = jnp.sum(jnp.where(rank == gy, row, 0.0), axis=1, keepdims=True)
    meta_ref[...] = jnp.where(iota((8, LANES), 0) == 0, begin, held).astype(I32)

    gain_ref[...] = gains(jnp.concatenate([column(ext_ref[8], x) for x in range(8)], axis=0), pieces)


def sweep_kernel(ext_ref, first_ref, second_ref, pieces_ref, gain_ref, smooth_ref, out_ref):
    shape = (16, LANES)
    lane = iota(shape, 1)
    first, last = lane == 0, lane == LANES - 1
    even = lax.axis_index("gx") % 2 == 0
    one, two = first_ref[...], second_ref[...]
    west, east = jnp.where(even, two, one), jnp.where(even, one, two)
    own_columns = [column(ext_ref[8], x) for x in range(8)]
    ids = [column(west[10], step) for step in range(5)] + [column(east[10], step) for step in range(5)]
    beside = gains(jnp.concatenate(ids, axis=0), pieces_ref[...])

    conduct, source, heat, own_sides = {}, {}, {}, {}
    for x in range(8):
        wide = ext_ref[x] * gain_ref[24 * x : 24 * x + 24]
        conduct[x] = wide[4:20]
        own_sides[x] = wide[3:19] + wide[5:21]
        source[x] = ext_ref[9 + x, 0:16]
        heat[x] = ext_ref[17 + x, 0:16]
    for step in range(5):
        conduct[step - 5] = west[step] * beside[16 * step : 16 * step + 16]
        conduct[step + 8] = east[step] * beside[80 + 16 * step : 96 + 16 * step]
    for step in range(4):
        source[step - 4] = west[5 + step]
        source[step + 8] = east[5 + step]
    heat[-1] = west[9]
    heat[8] = east[9]

    def depth_sides(v):
        up = jnp.where(first, 0.0, pltpu.roll(v, 1, 1))
        down = jnp.where(last, 0.0, pltpu.roll(v, LANES - 1, 1))
        return up, down

    def north_sides(v):
        return pltpu.roll(v, 1, 0), pltpu.roll(v, 15, 0)

    def around(rows, x):
        v = rows[x]
        up, down = depth_sides(v)
        south, north = north_sides(v)
        return ((rows[x - 1] + rows[x + 1]) + (south + north)) + (up + down)

    inverse, dual = {}, {}
    for x in range(-4, 12):
        v = conduct[x]
        if 0 <= x < 8:
            across = own_sides[x]
        else:
            south, north = north_sides(v)
            across = south + north
        up, down = depth_sides(v)
        twice = 6.0 * v + (((conduct[x - 1] + conduct[x + 1]) + across) + (up + down))
        inverse[x] = jnp.where(v > 0.0, 2.0 / twice, 0.0)
        dual[x] = source[x] * inverse[x]
    for sweep in range(ITERS):
        reach = 3 - sweep
        flux = {x: conduct[x] * dual[x] for x in dual}
        fresh = {}
        for x in range(-reach, 8 + reach):
            coupled = 0.5 * (conduct[x] * around(dual, x) + around(flux, x))
            fresh[x] = (1.0 - RELAXATION) * dual[x] + (RELAXATION * inverse[x]) * (source[x] + coupled)
        dual = fresh
    blocks = []
    for x in range(8):
        t, v = heat[x], dual[x]
        total = (t - heat[x + 1]) * (v - dual[x + 1]) + (t - heat[x - 1]) * (v - dual[x - 1])
        for near_t, near_v in zip(north_sides(t) + depth_sides(t), north_sides(v) + depth_sides(v)):
            total = total + (t - near_t) * (v - near_v)
        blocks.append(((-0.5 * SENS_SCALE) * total * conduct[x])[4:12])
    stacked = jnp.concatenate(blocks + [own[8:16] for own in own_columns], axis=0)
    turned = jnp.transpose(stacked)
    sums = jnp.sum(turned, axis=0, keepdims=True)
    row = jnp.where(iota((1, LANES), 1) < 64, sums, turned[0:1])
    odd = (iota((8, LANES), 0) & 1) == 1
    for owner in range(smooth_ref.shape[0]):
        out_ref[8 * owner : 8 * owner + 8] = jnp.where(odd, smooth_ref[owner : owner + 1], row)


def place_kernel(meta_ref, all_ref, out_ref, smooth_ref):
    start, held = meta_ref[0, 0], meta_ref[1, 0]
    sources = all_ref.shape[0] // 2
    half = sources // 2
    both = all_ref[pl.ds(0, sources, stride=2), :]
    turned = pltpu.roll(both, 64, 1)
    left = iota((half, LANES), 1) < 64
    values = jnp.where(left, both[:half], turned[half:])
    slots = jnp.where(left, turned[:half], both[half:]).astype(I32) - start
    pieces = [piece.astype(F32) for piece in thirds(values)]
    slot_rows = out_ref.shape[0]
    high = jnp.clip(slots >> 7, -1, slot_rows).astype(F32)
    low = (slots & 127).astype(F32)
    high_row = iota((slot_rows, LANES), 0).astype(F32).astype(BF16)
    low_row = iota((LANES, LANES), 0).astype(F32).astype(BF16)
    one, zero = jnp.ones((), BF16), jnp.zeros((), BF16)

    def spread(rows, row, count):
        sixteen = jnp.broadcast_to(rows[row : row + 1], (16, LANES)).astype(BF16)
        return jnp.concatenate([sixteen] * (count // 16), axis=0)

    sums = jnp.zeros((3 * slot_rows, LANES), F32)
    for pair in range(half // 2):
        hot, place = [], []
        for row in (2 * pair, 2 * pair + 1):
            match = high_row == spread(high, row, slot_rows)
            hot.append(jnp.concatenate([jnp.where(match, spread(piece, row, slot_rows), zero) for piece in pieces], axis=0))
            place.append(jnp.where(low_row == spread(low, row, LANES), one, zero))
        hot, place = jnp.concatenate(hot, axis=1), jnp.concatenate(place, axis=1)
        sums = sums + lax.dot_general(hot, place, (((1,), (1,)), ((), ())), preferred_element_type=F32)
    sums = sums[0:slot_rows] + sums[slot_rows : 2 * slot_rows] + sums[2 * slot_rows :]

    terms = all_ref[pl.ds(1, sources, stride=2), :].reshape(sources // 8, 8, LANES)
    group, source = iota((1, 8, LANES), 2) >> 4, iota((1, 8, LANES), 1)
    first = jnp.sum(jnp.where(group == source, terms, 0.0), axis=1)
    second = pltpu.roll(jnp.sum(jnp.where(group == ((source + 4) & 7), terms, 0.0), axis=1), 64, 1)
    for copy in range(2):
        smooth_ref[32 * copy : 32 * copy + 16] = first
        smooth_ref[32 * copy + 16 : 32 * copy + 32] = second
    smooth_ref[64:72] = first[0:8]
    top, shift = (start >> 7) & 31, start & 127
    moved = pltpu.roll(smooth_ref[pl.ds(top, 40), :], LANES - shift, 1)
    lane = iota((slot_rows, LANES), 1)
    smooth = jnp.where(lane < LANES - shift, moved[0:slot_rows], moved[1 : slot_rows + 1])
    within = iota((slot_rows, LANES), 0) * LANES + lane
    out_ref[...] = jnp.where(within < held, sums + smooth, 0.0)


def swap(array, axis, begin):
    pairs = [(i, i + 1) for i in range(begin, lax.axis_size(axis) - 1, 2)]
    return lax.ppermute(array, axis, pairs + [(b, a) for a, b in pairs])


def body(temp, rock, misfit, zone_map, zone_log, tally, adjacency):
    east, north, depth = temp.shape
    across, along = lax.axis_size("gx"), lax.axis_size("gy")
    devices = across * along
    shard_rows = zone_log.shape[0] // LANES
    zone = zone_log.reshape(shard_rows, LANES)
    shape = jax.ShapeDtypeStruct
    pack, counts, spread = call(
        pack_kernel,
        [
            shape((3 * east + 1, north, depth), F32),
            shape((1, along), I32),
            shape((along * ROWS, LANES), F32),
        ],
        [HBM] * 7,
        [
            pltpu.VMEM((east, 1, north), I32),
            pltpu.VMEM((shard_rows, LANES), F32),
            pltpu.VMEM((NBRS, zone_log.shape[0]), I32),
            pltpu.VMEM((8 * shard_rows, LANES), F32),
            pltpu.VMEM((along * ROWS, LANES), F32),
            pltpu.SemaphoreType.DMA((8,)),
        ],
        out_specs=[VMEM, VMEM, HBM],
    )(
        *map(
            in_hbm,
            (
                temp,
                rock,
                misfit,
                jnp.transpose(zone_map, (0, 2, 1)),
                zone,
                jnp.transpose(adjacency),
                tally.reshape(1, along),
            ),
        )
    )
    y_first, y_second = swap(pack, "gy", 0), swap(pack, "gy", 1)
    spread, y_first = lax.optimization_barrier((spread, y_first))
    shards = lax.all_to_all(spread.reshape(along, 1, ROWS * LANES), "gy", 0, 0, tiled=True).reshape(along * ROWS, LANES)
    ext, slab_a, slab_b = call(
        extend_kernel,
        [shape((25, 24, LANES), F32), shape((11, 16, LANES), F32), shape((11, 16, LANES), F32)],
        [VMEM] * 3,
        cost=pl.CostEstimate(flops=1 << 37, bytes_accessed=1 << 20, transcendentals=0),
    )(pack, y_first, y_second)
    x_first, x_second = swap(slab_a, "gx", 0), swap(slab_b, "gx", 1)
    smooth, meta, pieces, gain = call(
        smooth_kernel,
        [
            shape((along, LANES), F32),
            shape((8, LANES), I32),
            shape((3 * LANES, along * shard_rows), BF16),
            shape((east * 24, LANES), F32),
        ],
        [VMEM] * 3,
        [pltpu.VMEM((along, LANES), F32)],
        cost=pl.CostEstimate(flops=1 << 32, bytes_accessed=1 << 20, transcendentals=0),
    )(shards, ext, counts)
    rows = call(sweep_kernel, shape((devices * 2, LANES), F32), [VMEM] * 6)(ext, x_first, x_second, pieces, gain, smooth)
    gathered = lax.all_to_all(rows.reshape(devices, 1, 2 * LANES), ("gy", "gx"), 0, 0, tiled=True)
    slot_rows = 2 * shard_rows
    out = call(
        place_kernel,
        shape((slot_rows, LANES), F32),
        [VMEM, VMEM],
        [pltpu.VMEM((72, LANES), F32)],
    )(meta, gathered.reshape(devices * 2, LANES))
    return out.reshape(slot_rows * LANES)


def solution(mesh):
    placed = (
        P("gx", "gy", None),
        P("gx", "gy", None),
        P("gx", "gy", None),
        P("gx", "gy", None),
        P("gy"),
        P(),
        P("gy", None),
    )
    return jax.shard_map(body, mesh=mesh, in_specs=placed, out_specs=P("gy"), check_vma=False)
```

```python
import jax
import jax.numpy as jnp
from jax import lax
from jax.experimental import pallas as pl
from jax.experimental.pallas import tpu as pltpu
from jax.sharding import PartitionSpec as P

NBRS = 6
ITERS = 3
RELAXATION = 0.8
SMOOTHING = 0.5
SENS_SCALE = 0.03125
LANES = 128
X, Y, ALL = "x", ("y", "z", "core"), ("core", "z", "y", "x")
ROWS = 17
F32 = jnp.float32
BF16 = jnp.bfloat16
I32 = jnp.int32

VMEM = pl.BlockSpec(memory_space=pltpu.VMEM)
HBM = pl.BlockSpec(memory_space=pltpu.HBM)


def iota(shape, dim):
    return lax.broadcasted_iota(I32, shape, dim)


def in_hbm(array):
    return pltpu.with_memory_space_constraint(array, pltpu.HBM)


def call(kernel, outs, in_specs, scratch=(), cost=None, out_specs=None):
    one = not isinstance(outs, (list, tuple))
    shapes = [outs] if one else list(outs)
    return pl.pallas_call(
        kernel,
        out_shape=shapes[0] if one else shapes,
        in_specs=in_specs,
        out_specs=out_specs or (VMEM if one else [VMEM] * len(shapes)),
        scratch_shapes=list(scratch),
        cost_estimate=cost,
        compiler_params=pltpu.CompilerParams(vmem_limit_bytes=32 << 20),
    )


def thirds(table):
    first = table.astype(BF16)
    rest = table - first.astype(F32)
    second = rest.astype(BF16)
    third = (rest - second.astype(F32)).astype(BF16)
    return first, second, third


def column(tile, lane):
    picked = jnp.where(iota(tile.shape, 1) == lane, tile, 0.0)
    return jnp.broadcast_to(jnp.sum(picked, axis=1, keepdims=True), tile.shape)


def owner_of(number):
    core, z, y = number // 16, number // 4 % 4, number % 4
    return (y * 4 + z) * 2 + core


def pack_kernel(
    temp_ref, rock_ref, misfit_ref, map_ref, zone_ref, near_ref, tally_ref,
    pack_ref, counts_ref, spread_ref, map_buf, shard_ref, table_ref, lists_ref, many_ref, sems,
):
    east, north = rock_ref.shape[0], rock_ref.shape[1]
    copies = [
        pltpu.make_async_copy(source, target, sems.at[number])
        for number, (source, target) in enumerate(
            [
                (near_ref, table_ref),
                (zone_ref, shard_ref),
                (map_ref, map_buf),
                (rock_ref, pack_ref.at[pl.ds(0, east)]),
                (misfit_ref, pack_ref.at[pl.ds(east, east)]),
                (temp_ref, pack_ref.at[pl.ds(2 * east, east)]),
                (tally_ref, counts_ref),
                (many_ref, spread_ref),
            ]
        )
    ]
    for copy in copies[:-1]:
        copy.start()
    copies[0].wait()
    tiles = table_ref.shape[1] // LANES
    for tile in range(tiles):
        lists_ref[8 * tile : 8 * tile + NBRS] = table_ref[:, tile * LANES : (tile + 1) * LANES].astype(F32)
    group = iota((tiles, LANES), 1) >> 4
    first = lax.axis_index(X) * 16
    for odd in range(2):
        ids = jnp.zeros((tiles, LANES), F32)
        for number in range(NBRS):
            moved = pltpu.roll(
                lists_ref[pl.ds(number, tiles, stride=8), :], (2 * LANES + 16 * number - 64 * odd - first) & 127, 1
            )
            ids = jnp.where(group == number, moved, ids)
        for tile in range(tiles):
            place = ROWS * owner_of(2 * tile + odd) + 16
            many_ref[place : place + 1] = ids[tile : tile + 1]
    copies[1].wait()
    shard = shard_ref[...]
    for other in range(2 * tiles):
        many_ref[other * ROWS : other * ROWS + 16] = shard
    copies[-1].start()
    copies[2].wait()
    diagonal = iota((north, north), 0) == iota((north, north), 1)
    lane = iota((north, LANES), 1)
    ids = jnp.zeros((north, LANES), F32)
    for x in range(east):
        row = jnp.broadcast_to(map_buf[x].astype(F32), (north, north))
        one = jnp.sum(jnp.where(diagonal, row, 0.0), axis=1, keepdims=True)
        ids = jnp.where(lane == x, one, ids)
    pack_ref[3 * east] = ids
    for copy in copies[3:]:
        copy.wait()


def extend_kernel(own_ref, first_ref, second_ref, ext_ref, slab_a_ref, slab_b_ref):
    gx, gy = lax.axis_index(X), lax.axis_index(Y)
    even = gy % 2 == 0

    def window(begin, count):
        one, two = first_ref[begin : begin + count], second_ref[begin : begin + count]
        south, north = jnp.where(even, two, one), jnp.where(even, one, two)
        return jnp.concatenate([south, own_ref[begin : begin + count], north], axis=1)

    rock, ids = window(0, 8), window(24, 1)
    misfit, temp = window(8, 8)[:, 4:20], window(16, 8)[:, 4:20]
    ext_ref[0:8] = rock
    ext_ref[8:9] = ids
    ext_ref[9:17, 0:16] = misfit
    ext_ref[17:25, 0:16] = temp
    inner, ids = rock[:, 4:20], ids[:, 4:20]
    low = (inner[0:5], misfit[0:4], temp[0:1], ids)
    moved = pltpu.roll(ids[0], LANES - 3, 1).reshape(1, 16, LANES)
    high = (inner[3:8], misfit[4:8], temp[7:8], moved)
    east_first = gx % 2 == 0
    begin = 0
    for lower, upper in zip(low, high):
        end = begin + lower.shape[0]
        slab_a_ref[begin:end] = jnp.where(east_first, upper, lower)
        slab_b_ref[begin:end] = jnp.where(east_first, lower, upper)
        begin = end


def gains(ids, pieces):
    ids = ids.astype(I32)
    rows, lanes = ids >> 7, iota(ids.shape, 1)
    hot = jnp.concatenate(
        [jnp.where(rows == lanes + LANES * part, 1.0, 0.0).astype(BF16) for part in range(pieces.shape[1] // LANES)], axis=1
    )
    found = lax.dot_general(hot, pieces, (((1,), (1,)), ((), ())), preferred_element_type=F32)
    found = found[:, 0:LANES] + found[:, LANES : 2 * LANES] + found[:, 2 * LANES :]
    log = jnp.sum(jnp.where(lanes == (ids & 127), found, 0.0), axis=1, keepdims=True)
    return jnp.exp(jnp.broadcast_to(log, ids.shape))


def smooth_kernel(all_ref, ext_ref, tally_ref, out_ref, meta_ref, pieces_ref, gain_ref, term_ref):
    gy, number = lax.axis_index(Y), lax.axis_index(ALL)
    shards = all_ref.shape[0] // ROWS
    table = jnp.concatenate([all_ref[ROWS * shard : ROWS * shard + 16] for shard in range(shards)], axis=0)
    high_size = table.shape[0]
    pieces = jnp.concatenate(thirds(jnp.transpose(table)), axis=0)
    pieces_ref[...] = pieces

    lane = iota((24, LANES), 1)
    ids = all_ref[pl.ds(16, shards, stride=ROWS), :]
    rest = jnp.concatenate([pltpu.roll(ids[24:], 96 - 32 * part, 1) for part in range(3)], axis=0)
    ids = jnp.where(lane < 96, ids[:24], rest).astype(I32)
    high, low = ids >> 7, ids & 127
    high_row = iota((high_size, LANES), 0)
    low_row = iota((LANES, LANES), 0)
    near = []
    for chunk in range(6):
        rows = range(4 * chunk, 4 * chunk + 4)
        hot = jnp.concatenate(
            [jnp.where(high_row == high[row : row + 1], 1.0, 0.0).astype(BF16) for row in rows], axis=1
        )
        found = jnp.dot(pieces, hot, preferred_element_type=F32)
        found = found[0:LANES] + found[LANES : 2 * LANES] + found[2 * LANES :]
        for block, row in enumerate(rows):
            picked = jnp.where(low_row == low[row : row + 1], found[:, block * LANES : (block + 1) * LANES], 0.0)
            near.append(jnp.sum(picked, axis=0, keepdims=True))
    near = jnp.concatenate(near, axis=0)
    lane = iota((8, LANES), 1)
    rest = jnp.zeros((8, LANES), F32)
    for part in range(3):
        moved = pltpu.roll(near[8 * part : 8 * part + 8], 32 + 32 * part, 1)
        rest = jnp.where((lane >> 5) == part, moved, rest)
    near = jnp.concatenate([near, rest], axis=0)
    total = near
    for entry in range(1, NBRS):
        total = total + pltpu.roll(near, LANES - 16 * entry, 1)
    mine = number & 7
    own = all_ref[pl.ds(number >> 3, shards, stride=ROWS), :]
    own = pltpu.roll(own, (LANES - mine * 16) & 127, 1)
    term_ref[...] = SMOOTHING * (NBRS * own - total)

    lane = iota((16, LANES), 1)
    first = pltpu.roll(term_ref[pl.ds(0, 16, stride=2), :], mine * 16, 1)
    second = pltpu.roll(term_ref[pl.ds(1, 16, stride=2), :], (mine * 16 + 64) & 127, 1)
    terms = jnp.where((lane >> 4) == mine, first, jnp.where((lane >> 4) == ((mine + 4) & 7), second, 0.0))

    owners = tally_ref.shape[1]
    tally = jnp.broadcast_to(tally_ref[...].astype(F32), (owners, owners))
    before = iota((owners, owners), 1) < iota((owners, owners), 0)
    start = jnp.sum(jnp.where(before, tally, 0.0), axis=1, keepdims=True)
    start = jnp.broadcast_to(start, (owners, LANES)).astype(I32)
    lane = iota((owners, LANES), 1)
    slot = jnp.where((lane >> 4) == mine, 0, 2048) + number * 16 + (lane & 15)
    wanted = (start >> 12) + jnp.where(slot < (start & 4095), 1, 0)
    chosen = jnp.zeros((owners, LANES), F32)
    for window in range(16):
        chosen = chosen + jnp.where(wanted == window, terms[window : window + 1], 0.0)
    out_ref[...] = chosen

    row = tally[0:1]
    rank = iota(row.shape, 1)
    begin = jnp.sum(jnp.where(rank < gy, row, 0.0), axis=1, keepdims=True)
    held = jnp.sum(jnp.where(rank == gy, row, 0.0), axis=1, keepdims=True)
    meta_ref[...] = jnp.where(iota((8, LANES), 0) == 0, begin, held).astype(I32)

    gain_ref[...] = gains(jnp.concatenate([column(ext_ref[8], x) for x in range(8)], axis=0), pieces)


def sweep_kernel(ext_ref, first_ref, second_ref, pieces_ref, gain_ref, smooth_ref, out_ref):
    shape = (16, LANES)
    lane = iota(shape, 1)
    first, last = lane == 0, lane == LANES - 1
    even = lax.axis_index(X) % 2 == 0
    one, two = first_ref[...], second_ref[...]
    west, east = jnp.where(even, two, one), jnp.where(even, one, two)
    own_columns = [column(ext_ref[8], x) for x in range(8)]
    ids = [column(west[10], step) for step in range(5)] + [column(east[10], step) for step in range(5)]
    beside = gains(jnp.concatenate(ids, axis=0), pieces_ref[...])

    conduct, source, heat, own_sides = {}, {}, {}, {}
    for x in range(8):
        wide = ext_ref[x] * gain_ref[24 * x : 24 * x + 24]
        conduct[x] = wide[4:20]
        own_sides[x] = wide[3:19] + wide[5:21]
        source[x] = ext_ref[9 + x, 0:16]
        heat[x] = ext_ref[17 + x, 0:16]
    for step in range(5):
        conduct[step - 5] = west[step] * beside[16 * step : 16 * step + 16]
        conduct[step + 8] = east[step] * beside[80 + 16 * step : 96 + 16 * step]
    for step in range(4):
        source[step - 4] = west[5 + step]
        source[step + 8] = east[5 + step]
    heat[-1] = west[9]
    heat[8] = east[9]

    def depth_sides(v):
        up = jnp.where(first, 0.0, pltpu.roll(v, 1, 1))
        down = jnp.where(last, 0.0, pltpu.roll(v, LANES - 1, 1))
        return up, down

    def north_sides(v):
        return pltpu.roll(v, 1, 0), pltpu.roll(v, 15, 0)

    def around(rows, x):
        v = rows[x]
        up, down = depth_sides(v)
        south, north = north_sides(v)
        return ((rows[x - 1] + rows[x + 1]) + (south + north)) + (up + down)

    inverse, dual = {}, {}
    for x in range(-4, 12):
        v = conduct[x]
        if 0 <= x < 8:
            across = own_sides[x]
        else:
            south, north = north_sides(v)
            across = south + north
        up, down = depth_sides(v)
        twice = 6.0 * v + (((conduct[x - 1] + conduct[x + 1]) + across) + (up + down))
        inverse[x] = jnp.where(v > 0.0, 2.0 / twice, 0.0)
        dual[x] = source[x] * inverse[x]
    for sweep in range(ITERS):
        reach = 3 - sweep
        flux = {x: conduct[x] * dual[x] for x in dual}
        fresh = {}
        for x in range(-reach, 8 + reach):
            coupled = 0.5 * (conduct[x] * around(dual, x) + around(flux, x))
            fresh[x] = (1.0 - RELAXATION) * dual[x] + (RELAXATION * inverse[x]) * (source[x] + coupled)
        dual = fresh
    blocks = []
    for x in range(8):
        t, v = heat[x], dual[x]
        total = (t - heat[x + 1]) * (v - dual[x + 1]) + (t - heat[x - 1]) * (v - dual[x - 1])
        for near_t, near_v in zip(north_sides(t) + depth_sides(t), north_sides(v) + depth_sides(v)):
            total = total + (t - near_t) * (v - near_v)
        blocks.append(((-0.5 * SENS_SCALE) * total * conduct[x])[4:12])
    stacked = jnp.concatenate(blocks + [own[8:16] for own in own_columns], axis=0)
    turned = jnp.transpose(stacked)
    sums = jnp.sum(turned, axis=0, keepdims=True)
    row = jnp.where(iota((1, LANES), 1) < 64, sums, turned[0:1])
    odd = (iota((8, LANES), 0) & 1) == 1
    for four in range(smooth_ref.shape[0]):
        owner = owner_of(four)
        out_ref[8 * four : 8 * four + 8] = jnp.where(odd, smooth_ref[owner : owner + 1], row)


def place_kernel(meta_ref, all_ref, out_ref, smooth_ref):
    start, held = meta_ref[0, 0], meta_ref[1, 0]
    sources = all_ref.shape[0] // 2
    half = sources // 2
    both = all_ref[pl.ds(0, sources, stride=2), :]
    turned = pltpu.roll(both, 64, 1)
    left = iota((half, LANES), 1) < 64
    values = jnp.where(left, both[:half], turned[half:])
    slots = jnp.where(left, turned[:half], both[half:]).astype(I32) - start
    pieces = [piece.astype(F32) for piece in thirds(values)]
    slot_rows = out_ref.shape[0]
    high = jnp.clip(slots >> 7, -1, slot_rows).astype(F32)
    low = (slots & 127).astype(F32)
    high_row = iota((slot_rows, LANES), 0).astype(F32).astype(BF16)
    low_row = iota((LANES, LANES), 0).astype(F32).astype(BF16)
    one, zero = jnp.ones((), BF16), jnp.zeros((), BF16)

    def spread(rows, row, count):
        sixteen = jnp.broadcast_to(rows[row : row + 1], (16, LANES)).astype(BF16)
        return jnp.concatenate([sixteen] * (count // 16), axis=0)

    sums = jnp.zeros((3 * slot_rows, LANES), F32)
    for pair in range(half // 2):
        hot, place = [], []
        for row in (2 * pair, 2 * pair + 1):
            match = high_row == spread(high, row, slot_rows)
            hot.append(jnp.concatenate([jnp.where(match, spread(piece, row, slot_rows), zero) for piece in pieces], axis=0))
            place.append(jnp.where(low_row == spread(low, row, LANES), one, zero))
        hot, place = jnp.concatenate(hot, axis=1), jnp.concatenate(place, axis=1)
        sums = sums + lax.dot_general(hot, place, (((1,), (1,)), ((), ())), preferred_element_type=F32)
    sums = sums[0:slot_rows] + sums[slot_rows : 2 * slot_rows] + sums[2 * slot_rows :]

    terms = all_ref[pl.ds(1, sources, stride=2), :].reshape(sources // 8, 8, LANES)
    group, source = iota((1, 8, LANES), 2) >> 4, iota((1, 8, LANES), 1)
    first = jnp.sum(jnp.where(group == source, terms, 0.0), axis=1)
    second = pltpu.roll(jnp.sum(jnp.where(group == ((source + 4) & 7), terms, 0.0), axis=1), 64, 1)
    for copy in range(2):
        smooth_ref[32 * copy : 32 * copy + 16] = first
        smooth_ref[32 * copy + 16 : 32 * copy + 32] = second
    smooth_ref[64:72] = first[0:8]
    top, shift = (start >> 7) & 31, start & 127
    moved = pltpu.roll(smooth_ref[pl.ds(top, 40), :], LANES - shift, 1)
    lane = iota((slot_rows, LANES), 1)
    smooth = jnp.where(lane < LANES - shift, moved[0:slot_rows], moved[1 : slot_rows + 1])
    within = iota((slot_rows, LANES), 0) * LANES + lane
    out_ref[...] = jnp.where(within < held, sums + smooth, 0.0)


def swap(array, axis, begin):
    pairs = [(i, i + 1) for i in range(begin, lax.axis_size(axis) - 1, 2)]
    return lax.ppermute(array, axis, pairs + [(b, a) for a, b in pairs])


def body(temp, rock, misfit, zone_map, zone_log, tally, adjacency):
    east, north, depth = temp.shape
    across, along = lax.axis_size(X), lax.axis_size(Y)
    devices = across * along
    shard_rows = zone_log.shape[0] // LANES
    zone = zone_log.reshape(shard_rows, LANES)
    shape = jax.ShapeDtypeStruct
    pack, counts, spread = call(
        pack_kernel,
        [
            shape((3 * east + 1, north, depth), F32),
            shape((1, along), I32),
            shape((along * ROWS, LANES), F32),
        ],
        [HBM] * 7,
        [
            pltpu.VMEM((east, 1, north), I32),
            pltpu.VMEM((shard_rows, LANES), F32),
            pltpu.VMEM((NBRS, zone_log.shape[0]), I32),
            pltpu.VMEM((8 * shard_rows, LANES), F32),
            pltpu.VMEM((along * ROWS, LANES), F32),
            pltpu.SemaphoreType.DMA((8,)),
        ],
        out_specs=[VMEM, VMEM, HBM],
    )(
        *map(
            in_hbm,
            (
                temp,
                rock,
                misfit,
                jnp.transpose(zone_map, (0, 2, 1)),
                zone,
                jnp.transpose(adjacency),
                tally.reshape(1, along),
            ),
        )
    )
    y_first, y_second = swap(pack, Y, 0), swap(pack, Y, 1)
    spread, y_first = lax.optimization_barrier((spread, y_first))
    shards = lax.all_to_all(spread.reshape(along, 1, ROWS * LANES), Y, 0, 0, tiled=True).reshape(along * ROWS, LANES)
    ext, slab_a, slab_b = call(
        extend_kernel,
        [shape((25, 24, LANES), F32), shape((11, 16, LANES), F32), shape((11, 16, LANES), F32)],
        [VMEM] * 3,
        cost=pl.CostEstimate(flops=1 << 37, bytes_accessed=1 << 20, transcendentals=0),
    )(pack, y_first, y_second)
    x_first, x_second = swap(slab_a, X, 0), swap(slab_b, X, 1)
    smooth, meta, pieces, gain = call(
        smooth_kernel,
        [
            shape((along, LANES), F32),
            shape((8, LANES), I32),
            shape((3 * LANES, along * shard_rows), BF16),
            shape((east * 24, LANES), F32),
        ],
        [VMEM] * 3,
        [pltpu.VMEM((along, LANES), F32)],
        cost=pl.CostEstimate(flops=1 << 32, bytes_accessed=1 << 20, transcendentals=0),
    )(shards, ext, counts)
    rows = call(sweep_kernel, shape((devices * 2, LANES), F32), [VMEM] * 6)(ext, x_first, x_second, pieces, gain, smooth)
    gathered = lax.all_to_all(rows.reshape(devices, 1, 2 * LANES), ALL, 0, 0, tiled=True)
    slot_rows = 2 * shard_rows
    out = call(
        place_kernel,
        shape((slot_rows, LANES), F32),
        [VMEM, VMEM],
        [pltpu.VMEM((72, LANES), F32)],
    )(meta, gathered.reshape(devices * 2, LANES))
    return out.reshape(slot_rows * LANES)


def solution(mesh):
    physical = jax.sharding.Mesh(mesh.devices.reshape(4, 4, 4, 2), ("x", "y", "z", "core"))
    placed = (P(X, Y, None),) * 4 + (P(Y), P(), P(Y, None))
    return jax.shard_map(body, mesh=physical, in_specs=placed, out_specs=P(Y), check_vma=False)
```

```python
import jax
import jax.numpy as jnp
from jax import lax
from jax.experimental import pallas as pl
from jax.experimental.pallas import tpu as pltpu
from jax.sharding import PartitionSpec as P

NBRS = 6
ITERS = 3
RELAXATION = 0.8
SMOOTHING = 0.5
SENS_SCALE = 0.03125
LANES = 128
X, Y, ALL = "x", ("y", "z", "core"), ("core", "z", "y", "x")
ROWS = 17
F32 = jnp.float32
BF16 = jnp.bfloat16
I32 = jnp.int32

VMEM = pl.BlockSpec(memory_space=pltpu.VMEM)
HBM = pl.BlockSpec(memory_space=pltpu.HBM)


def iota(shape, dim):
    return lax.broadcasted_iota(I32, shape, dim)


def in_hbm(array):
    return pltpu.with_memory_space_constraint(array, pltpu.HBM)


def call(kernel, outs, in_specs, scratch=(), cost=None, out_specs=None):
    one = not isinstance(outs, (list, tuple))
    shapes = [outs] if one else list(outs)
    return pl.pallas_call(
        kernel,
        out_shape=shapes[0] if one else shapes,
        in_specs=in_specs,
        out_specs=out_specs or (VMEM if one else [VMEM] * len(shapes)),
        scratch_shapes=list(scratch),
        cost_estimate=cost,
        compiler_params=pltpu.CompilerParams(vmem_limit_bytes=32 << 20),
    )


def thirds(table):
    first = table.astype(BF16)
    rest = table - first.astype(F32)
    second = rest.astype(BF16)
    third = (rest - second.astype(F32)).astype(BF16)
    return first, second, third


def column(tile, lane):
    picked = jnp.where(iota(tile.shape, 1) == lane, tile, 0.0)
    return jnp.broadcast_to(jnp.sum(picked, axis=1, keepdims=True), tile.shape)


def owner_of(number):
    core, z, y = number // 16, number // 4 % 4, number % 4
    return (y * 4 + z) * 2 + core


def pack_kernel(
    temp_ref, rock_ref, misfit_ref, map_ref, zone_ref, near_ref, tally_ref,
    pack_ref, counts_ref, spread_ref, map_buf, shard_ref, table_ref, lists_ref, many_ref, sems,
):
    east, north = rock_ref.shape[0], rock_ref.shape[1]
    copies = [
        pltpu.make_async_copy(source, target, sems.at[number])
        for number, (source, target) in enumerate(
            [
                (near_ref, table_ref),
                (zone_ref, shard_ref),
                (map_ref, map_buf),
                (rock_ref, pack_ref.at[pl.ds(0, east)]),
                (misfit_ref, pack_ref.at[pl.ds(east, east)]),
                (temp_ref, pack_ref.at[pl.ds(2 * east, east)]),
                (tally_ref, counts_ref),
                (many_ref, spread_ref),
            ]
        )
    ]
    for copy in copies[:-1]:
        copy.start()
    copies[0].wait()
    tiles = table_ref.shape[1] // LANES
    for tile in range(tiles):
        lists_ref[8 * tile : 8 * tile + NBRS] = table_ref[:, tile * LANES : (tile + 1) * LANES].astype(F32)
    group = iota((tiles, LANES), 1) >> 4
    first = lax.axis_index(X) * 16
    for odd in range(2):
        ids = jnp.zeros((tiles, LANES), F32)
        for number in range(NBRS):
            moved = pltpu.roll(
                lists_ref[pl.ds(number, tiles, stride=8), :], (2 * LANES + 16 * number - 64 * odd - first) & 127, 1
            )
            ids = jnp.where(group == number, moved, ids)
        for tile in range(tiles):
            place = ROWS * owner_of(2 * tile + odd) + 16
            many_ref[place : place + 1] = ids[tile : tile + 1]
    copies[1].wait()
    shard = shard_ref[...]
    for other in range(2 * tiles):
        many_ref[other * ROWS : other * ROWS + 16] = shard
    copies[-1].start()
    copies[2].wait()
    diagonal = iota((north, north), 0) == iota((north, north), 1)
    lane = iota((north, LANES), 1)
    ids = jnp.zeros((north, LANES), F32)
    for x in range(east):
        row = jnp.broadcast_to(map_buf[x].astype(F32), (north, north))
        one = jnp.sum(jnp.where(diagonal, row, 0.0), axis=1, keepdims=True)
        ids = jnp.where(lane == x, one, ids)
    pack_ref[3 * east] = ids
    for copy in copies[3:]:
        copy.wait()


def extend_kernel(own_ref, first_ref, second_ref, ext_ref, slab_a_ref, slab_b_ref):
    gx, gy = lax.axis_index(X), lax.axis_index(Y)
    even = gy % 2 == 0

    def window(begin, count):
        one, two = first_ref[begin : begin + count], second_ref[begin : begin + count]
        south, north = jnp.where(even, two, one), jnp.where(even, one, two)
        return jnp.concatenate([south, own_ref[begin : begin + count], north], axis=1)

    rock, ids = window(0, 8), window(24, 1)
    misfit, temp = window(8, 8)[:, 4:20], window(16, 8)[:, 4:20]
    ext_ref[0:8] = rock
    ext_ref[8:9] = ids
    ext_ref[9:17, 0:16] = misfit
    ext_ref[17:25, 0:16] = temp
    inner, ids = rock[:, 4:20], ids[:, 4:20]
    low = (inner[0:5], misfit[0:4], temp[0:1], ids)
    moved = pltpu.roll(ids[0], LANES - 3, 1).reshape(1, 16, LANES)
    high = (inner[3:8], misfit[4:8], temp[7:8], moved)
    east_first = gx % 2 == 0
    begin = 0
    for lower, upper in zip(low, high):
        end = begin + lower.shape[0]
        slab_a_ref[begin:end] = jnp.where(east_first, upper, lower)
        slab_b_ref[begin:end] = jnp.where(east_first, lower, upper)
        begin = end


def gains(ids, pieces):
    ids = ids.astype(I32)
    rows, lanes = ids >> 7, iota(ids.shape, 1)
    hot = jnp.concatenate(
        [jnp.where(rows == lanes + LANES * part, 1.0, 0.0).astype(BF16) for part in range(pieces.shape[1] // LANES)], axis=1
    )
    found = lax.dot_general(hot, pieces, (((1,), (1,)), ((), ())), preferred_element_type=F32)
    found = found[:, 0:LANES] + found[:, LANES : 2 * LANES] + found[:, 2 * LANES :]
    log = jnp.sum(jnp.where(lanes == (ids & 127), found, 0.0), axis=1, keepdims=True)
    return jnp.exp(jnp.broadcast_to(log, ids.shape))


def smooth_kernel(all_ref, ext_ref, tally_ref, out_ref, meta_ref, pieces_ref, gain_ref, term_ref):
    gy, number = lax.axis_index(Y), lax.axis_index(ALL)
    shards = all_ref.shape[0] // ROWS
    table = jnp.concatenate([all_ref[ROWS * shard : ROWS * shard + 16] for shard in range(shards)], axis=0)
    high_size = table.shape[0]
    parts = thirds(jnp.transpose(table))
    pieces = jnp.concatenate(parts, axis=0)
    pieces_ref[...] = pieces

    lane = iota((24, LANES), 1)
    ids = all_ref[pl.ds(16, shards, stride=ROWS), :]
    rest = jnp.concatenate([pltpu.roll(ids[24:], 96 - 32 * part, 1) for part in range(3)], axis=0)
    ids = jnp.where(lane < 96, ids[:24], rest).astype(I32)
    high, low = ids >> 7, ids & 127
    high_row = iota((high_size, LANES), 0)
    low_row = iota((LANES, LANES), 0)
    near = []
    for chunk in range(6):
        rows = range(4 * chunk, 4 * chunk + 4)
        hot = jnp.concatenate(
            [jnp.where(high_row == high[row : row + 1], 1.0, 0.0).astype(BF16) for row in rows], axis=1
        )
        found = sum(jnp.dot(piece, hot, preferred_element_type=F32) for piece in parts)
        for block, row in enumerate(rows):
            picked = jnp.where(low_row == low[row : row + 1], found[:, block * LANES : (block + 1) * LANES], 0.0)
            near.append(jnp.sum(picked, axis=0, keepdims=True))
    near = jnp.concatenate(near, axis=0)
    lane = iota((8, LANES), 1)
    rest = jnp.zeros((8, LANES), F32)
    for part in range(3):
        moved = pltpu.roll(near[8 * part : 8 * part + 8], 32 + 32 * part, 1)
        rest = jnp.where((lane >> 5) == part, moved, rest)
    near = jnp.concatenate([near, rest], axis=0)
    total = near
    for entry in range(1, NBRS):
        total = total + pltpu.roll(near, LANES - 16 * entry, 1)
    mine = number & 7
    own = all_ref[pl.ds(number >> 3, shards, stride=ROWS), :]
    own = pltpu.roll(own, (LANES - mine * 16) & 127, 1)
    term_ref[...] = SMOOTHING * (NBRS * own - total)

    lane = iota((16, LANES), 1)
    first = pltpu.roll(term_ref[pl.ds(0, 16, stride=2), :], mine * 16, 1)
    second = pltpu.roll(term_ref[pl.ds(1, 16, stride=2), :], (mine * 16 + 64) & 127, 1)
    terms = jnp.where((lane >> 4) == mine, first, jnp.where((lane >> 4) == ((mine + 4) & 7), second, 0.0))

    owners = tally_ref.shape[1]
    tally = jnp.broadcast_to(tally_ref[...].astype(F32), (owners, owners))
    before = iota((owners, owners), 1) < iota((owners, owners), 0)
    start = jnp.sum(jnp.where(before, tally, 0.0), axis=1, keepdims=True)
    start = jnp.broadcast_to(start, (owners, LANES)).astype(I32)
    lane = iota((owners, LANES), 1)
    slot = jnp.where((lane >> 4) == mine, 0, 2048) + number * 16 + (lane & 15)
    wanted = (start >> 12) + jnp.where(slot < (start & 4095), 1, 0)
    chosen = jnp.zeros((owners, LANES), F32)
    for window in range(16):
        chosen = chosen + jnp.where(wanted == window, terms[window : window + 1], 0.0)
    out_ref[...] = chosen

    row = tally[0:1]
    rank = iota(row.shape, 1)
    begin = jnp.sum(jnp.where(rank < gy, row, 0.0), axis=1, keepdims=True)
    held = jnp.sum(jnp.where(rank == gy, row, 0.0), axis=1, keepdims=True)
    meta_ref[...] = jnp.where(iota((8, LANES), 0) == 0, begin, held).astype(I32)

    gain_ref[...] = gains(jnp.concatenate([column(ext_ref[8], x) for x in range(8)], axis=0), pieces)


def sweep_kernel(ext_ref, first_ref, second_ref, pieces_ref, gain_ref, smooth_ref, out_ref):
    shape = (16, LANES)
    lane = iota(shape, 1)
    first, last = lane == 0, lane == LANES - 1
    even = lax.axis_index(X) % 2 == 0
    one, two = first_ref[...], second_ref[...]
    west, east = jnp.where(even, two, one), jnp.where(even, one, two)
    own_columns = [column(ext_ref[8], x) for x in range(8)]
    ids = [column(west[10], step) for step in range(5)] + [column(east[10], step) for step in range(5)]
    beside = gains(jnp.concatenate(ids, axis=0), pieces_ref[...])

    conduct, source, heat, own_sides = {}, {}, {}, {}
    for x in range(8):
        wide = ext_ref[x] * gain_ref[24 * x : 24 * x + 24]
        conduct[x] = wide[4:20]
        own_sides[x] = wide[3:19] + wide[5:21]
        source[x] = ext_ref[9 + x, 0:16]
        heat[x] = ext_ref[17 + x, 0:16]
    for step in range(5):
        conduct[step - 5] = west[step] * beside[16 * step : 16 * step + 16]
        conduct[step + 8] = east[step] * beside[80 + 16 * step : 96 + 16 * step]
    for step in range(4):
        source[step - 4] = west[5 + step]
        source[step + 8] = east[5 + step]
    heat[-1] = west[9]
    heat[8] = east[9]

    def depth_sides(v):
        up = jnp.where(first, 0.0, pltpu.roll(v, 1, 1))
        down = jnp.where(last, 0.0, pltpu.roll(v, LANES - 1, 1))
        return up, down

    def north_sides(v):
        return pltpu.roll(v, 1, 0), pltpu.roll(v, 15, 0)

    def around(rows, x):
        v = rows[x]
        up, down = depth_sides(v)
        south, north = north_sides(v)
        return ((rows[x - 1] + rows[x + 1]) + (south + north)) + (up + down)

    inverse, dual = {}, {}
    for x in range(-4, 12):
        v = conduct[x]
        if 0 <= x < 8:
            across = own_sides[x]
        else:
            south, north = north_sides(v)
            across = south + north
        up, down = depth_sides(v)
        twice = 6.0 * v + (((conduct[x - 1] + conduct[x + 1]) + across) + (up + down))
        inverse[x] = jnp.where(v > 0.0, 2.0 / twice, 0.0)
        dual[x] = source[x] * inverse[x]
    for sweep in range(ITERS):
        reach = 3 - sweep
        flux = {x: conduct[x] * dual[x] for x in dual}
        fresh = {}
        for x in range(-reach, 8 + reach):
            coupled = 0.5 * (conduct[x] * around(dual, x) + around(flux, x))
            fresh[x] = (1.0 - RELAXATION) * dual[x] + (RELAXATION * inverse[x]) * (source[x] + coupled)
        dual = fresh
    blocks = []
    for x in range(8):
        t, v = heat[x], dual[x]
        total = (t - heat[x + 1]) * (v - dual[x + 1]) + (t - heat[x - 1]) * (v - dual[x - 1])
        for near_t, near_v in zip(north_sides(t) + depth_sides(t), north_sides(v) + depth_sides(v)):
            total = total + (t - near_t) * (v - near_v)
        blocks.append(((-0.5 * SENS_SCALE) * total * conduct[x])[4:12])
    stacked = jnp.concatenate(blocks + [own[8:16] for own in own_columns], axis=0)
    turned = jnp.transpose(stacked)
    sums = jnp.sum(turned, axis=0, keepdims=True)
    row = jnp.where(iota((1, LANES), 1) < 64, sums, turned[0:1])
    odd = (iota((8, LANES), 0) & 1) == 1
    for four in range(smooth_ref.shape[0]):
        owner = owner_of(four)
        out_ref[8 * four : 8 * four + 8] = jnp.where(odd, smooth_ref[owner : owner + 1], row)


def place_kernel(meta_ref, all_ref, out_ref, smooth_ref):
    start, held = meta_ref[0, 0], meta_ref[1, 0]
    sources = all_ref.shape[0] // 2
    half = sources // 2
    both = all_ref[pl.ds(0, sources, stride=2), :]
    turned = pltpu.roll(both, 64, 1)
    left = iota((half, LANES), 1) < 64
    values = jnp.where(left, both[:half], turned[half:])
    slots = jnp.where(left, turned[:half], both[half:]).astype(I32) - start
    pieces = [piece.astype(F32) for piece in thirds(values)]
    slot_rows = out_ref.shape[0]
    high = jnp.clip(slots >> 7, -1, slot_rows).astype(F32)
    low = (slots & 127).astype(F32)
    high_row = iota((slot_rows, LANES), 0).astype(F32).astype(BF16)
    low_row = iota((LANES, LANES), 0).astype(F32).astype(BF16)
    one, zero = jnp.ones((), BF16), jnp.zeros((), BF16)

    def spread(rows, row, count):
        sixteen = jnp.broadcast_to(rows[row : row + 1], (16, LANES)).astype(BF16)
        return jnp.concatenate([sixteen] * (count // 16), axis=0)

    sums = jnp.zeros((3 * slot_rows, LANES), F32)
    for pair in range(half // 2):
        hot, place = [], []
        for row in (2 * pair, 2 * pair + 1):
            match = high_row == spread(high, row, slot_rows)
            hot.append(jnp.concatenate([jnp.where(match, spread(piece, row, slot_rows), zero) for piece in pieces], axis=0))
            place.append(jnp.where(low_row == spread(low, row, LANES), one, zero))
        hot, place = jnp.concatenate(hot, axis=1), jnp.concatenate(place, axis=1)
        sums = sums + lax.dot_general(hot, place, (((1,), (1,)), ((), ())), preferred_element_type=F32)
    sums = sums[0:slot_rows] + sums[slot_rows : 2 * slot_rows] + sums[2 * slot_rows :]

    terms = all_ref[pl.ds(1, sources, stride=2), :].reshape(sources // 8, 8, LANES)
    group, source = iota((1, 8, LANES), 2) >> 4, iota((1, 8, LANES), 1)
    first = jnp.sum(jnp.where(group == source, terms, 0.0), axis=1)
    second = pltpu.roll(jnp.sum(jnp.where(group == ((source + 4) & 7), terms, 0.0), axis=1), 64, 1)
    for copy in range(2):
        smooth_ref[32 * copy : 32 * copy + 16] = first
        smooth_ref[32 * copy + 16 : 32 * copy + 32] = second
    smooth_ref[64:72] = first[0:8]
    top, shift = (start >> 7) & 31, start & 127
    moved = pltpu.roll(smooth_ref[pl.ds(top, 40), :], LANES - shift, 1)
    lane = iota((slot_rows, LANES), 1)
    smooth = jnp.where(lane < LANES - shift, moved[0:slot_rows], moved[1 : slot_rows + 1])
    within = iota((slot_rows, LANES), 0) * LANES + lane
    out_ref[...] = jnp.where(within < held, sums + smooth, 0.0)


def swap(array, axis, begin):
    pairs = [(i, i + 1) for i in range(begin, lax.axis_size(axis) - 1, 2)]
    return lax.ppermute(array, axis, pairs + [(b, a) for a, b in pairs])


def body(temp, rock, misfit, zone_map, zone_log, tally, adjacency):
    east, north, depth = temp.shape
    across, along = lax.axis_size(X), lax.axis_size(Y)
    devices = across * along
    shard_rows = zone_log.shape[0] // LANES
    zone = zone_log.reshape(shard_rows, LANES)
    shape = jax.ShapeDtypeStruct
    pack, counts, spread = call(
        pack_kernel,
        [
            shape((3 * east + 1, north, depth), F32),
            shape((1, along), I32),
            shape((along * ROWS, LANES), F32),
        ],
        [HBM] * 7,
        [
            pltpu.VMEM((east, 1, north), I32),
            pltpu.VMEM((shard_rows, LANES), F32),
            pltpu.VMEM((NBRS, zone_log.shape[0]), I32),
            pltpu.VMEM((8 * shard_rows, LANES), F32),
            pltpu.VMEM((along * ROWS, LANES), F32),
            pltpu.SemaphoreType.DMA((8,)),
        ],
        out_specs=[VMEM, VMEM, HBM],
    )(
        *map(
            in_hbm,
            (
                temp,
                rock,
                misfit,
                jnp.transpose(zone_map, (0, 2, 1)),
                zone,
                jnp.transpose(adjacency),
                tally.reshape(1, along),
            ),
        )
    )
    y_first, y_second = swap(pack, Y, 0), swap(pack, Y, 1)
    spread, y_first = lax.optimization_barrier((spread, y_first))
    shards = lax.all_to_all(spread.reshape(along, 1, ROWS * LANES), Y, 0, 0, tiled=True).reshape(along * ROWS, LANES)
    ext, slab_a, slab_b = call(
        extend_kernel,
        [shape((25, 24, LANES), F32), shape((11, 16, LANES), F32), shape((11, 16, LANES), F32)],
        [VMEM] * 3,
        cost=pl.CostEstimate(flops=1 << 37, bytes_accessed=1 << 20, transcendentals=0),
    )(pack, y_first, y_second)
    x_first, x_second = swap(slab_a, X, 0), swap(slab_b, X, 1)
    smooth, meta, pieces, gain = call(
        smooth_kernel,
        [
            shape((along, LANES), F32),
            shape((8, LANES), I32),
            shape((3 * LANES, along * shard_rows), BF16),
            shape((east * 24, LANES), F32),
        ],
        [VMEM] * 3,
        [pltpu.VMEM((along, LANES), F32)],
        cost=pl.CostEstimate(flops=1 << 32, bytes_accessed=1 << 20, transcendentals=0),
    )(shards, ext, counts)
    rows = call(sweep_kernel, shape((devices * 2, LANES), F32), [VMEM] * 6)(ext, x_first, x_second, pieces, gain, smooth)
    gathered = lax.all_to_all(rows.reshape(devices, 1, 2 * LANES), ALL, 0, 0, tiled=True)
    slot_rows = 2 * shard_rows
    out = call(
        place_kernel,
        shape((slot_rows, LANES), F32),
        [VMEM, VMEM],
        [pltpu.VMEM((72, LANES), F32)],
    )(meta, gathered.reshape(devices * 2, LANES))
    return out.reshape(slot_rows * LANES)


def solution(mesh):
    physical = jax.sharding.Mesh(mesh.devices.reshape(4, 4, 4, 2), ("x", "y", "z", "core"))
    placed = (P(X, Y, None),) * 4 + (P(Y), P(), P(Y, None))
    return jax.shard_map(body, mesh=physical, in_specs=placed, out_specs=P(Y), check_vma=False)
```
